32 devices in a mesh: group: 2 (over x), cell: 16 (over z, y, core).
Axes of the slice: x: 2, y: 2, z: 4, core: 2. Of those that a mesh axis runs over, the one named last changes fastest.
Arguments:
- cell_factor: bfloat16 [32768, 128], P(('group', 'cell')), parts along dimension 0, may hold values from -6 to 6
- sched_factor: bfloat16 [16384, 128], P('group'), parts along dimension 0, may hold values from -6 to 6
- core_matrix: float32 [256, 128], P('group'), parts along dimension 0, may hold values from -0.03125 to 0.03125
- rate_table: bfloat16 [64, 128], replicated, may hold values from 0.5 to 2
- cell_well: int32 [32768], P(('group', 'cell')), parts along dimension 0, may hold values from 0 to 63
- sched_profile: int32 [16384], P('group'), parts along dimension 0, may hold values from 0 to 127
Outputs:
- basis_cells: float32 [32768, 256], P(('group', 'cell')), parts along dimension 0
- basis_sched: float32 [16384, 256], P(('group', 'cell')), parts along dimension 0
- core_out: float32 [512, 256], P('group'), parts along dimension 0
The draws below stay inside these ranges and needn't reach their ends.
There are 2 independent parts, one for each index of `group`. The reference program is written for one: setup_inputs(seed, part) draws one part's arguments, and reference() takes and returns one part's arrays. A program takes and returns all parts, laid end to end along the dimension named above; an argument that names none is the same for every part. Nothing has to cross between parts.
All inputs are finite; a program needn't handle non-finite values.
Results may differ from the reference program's by a relative error of at most 0.02.
Values may be sent and summed in bfloat16 or wider, within the bound.
No kernel may reach another device: no remote copies, remote signals or barrier semaphores. Data moves between devices by JAX's collectives and lax.ppermute only.
A program may use at most 128 MiB of HBM per device.

```python
import jax
import jax.numpy as jnp
from jax import lax

R = 128
P_SIZE = 128
W = 64
CELL_DEV = 1024
NS = 8192
NC = 16384


def plant(entries, own_key, least, top_value):
    longest = entries.shape.index(max(entries.shape))
    spots = []
    for shift in (0, 1):
        where = [jax.random.randint(jax.random.fold_in(own_key, axis), (), 0, length) for axis, length in enumerate(entries.shape)]
        where[longest] = (where[longest] + shift) % entries.shape[longest]
        spots.append(tuple(where))
    return entries.at[spots[0]].set(least).at[spots[1]].set(top_value)


def shard_levels(rng, dims, split, smallest, high):
    level = 1.0
    for position, shards_of in split:
        steps = jax.random.uniform(jax.random.fold_in(jax.random.fold_in(rng, 6), position), (shards_of,), jnp.float32, smallest / len(split), high / len(split))
        level = level * jnp.repeat(jnp.exp(steps), dims[position] // shards_of).reshape((-1,) + (1,) * (len(dims) - 1 - position))
    return level


def noise(rng, dims, width, bound, split=(), held_as=jnp.bfloat16):
    values = width * jax.random.normal(rng, dims, jnp.float32)
    if split:
        values = values * shard_levels(rng, dims, split, -0.22, 0.18)
    return jnp.clip(values, -bound, bound).astype(held_as)


def setup_inputs(seed: int = 0, part: int = 0) -> dict:
    seeds = jax.random.split(jax.random.key(seed), 7)
    part_splits = jax.random.split(jax.random.fold_in(seeds[6], part), 7)
    return {
        "cell_factor": noise(part_splits[0], (NC, R), 1.0, 6.0, ((0, 16),)),
        "sched_factor": noise(part_splits[1], (NS, R), 1.0, 6.0),
        "core_matrix": noise(part_splits[2], (R, R), (1.0 / R), 0.03125, (), jnp.float32),
        "rate_table": jnp.clip(jax.random.uniform(seeds[3], (W, P_SIZE), jnp.float32, 0.5, 2.0), 0.5, 2.0).astype(jnp.bfloat16),
        "cell_well": plant(jax.random.randint(part_splits[4], (NC,), 0, W), jax.random.fold_in(part_splits[4], 1), 0, W - 1).astype(jnp.int32),
        "sched_profile": plant(jax.random.randint(part_splits[5], (NS,), 0, P_SIZE), jax.random.fold_in(part_splits[5], 1), 0, P_SIZE - 1).astype(jnp.int32),
    }


TIME_STEP = 0.25
PANEL_SCALE = 8.0

def local_gram(panel):
    return lax.dot_general(panel, panel, (((0,), (0,)), ((), ())), precision=lax.Precision.HIGHEST)

def orth_step(panel, gram):
    factor_low = jnp.linalg.cholesky(gram)
    return lax.linalg.triangular_solve(factor_low, panel, left_side=False, lower=True, transpose_a=True)

def orthonormal(panel):
    return orth_step(panel, local_gram(panel))

def build_tile(cell_rows, cell_wells, sched_factor, core_matrix, rate_table, prof_onehot):
    factor_mix = jnp.dot(cell_rows.astype(jnp.float32), core_matrix, precision=lax.Precision.HIGHEST).astype(jnp.bfloat16)
    rebuilt = lax.dot_general(factor_mix.astype(jnp.float32), sched_factor.astype(jnp.float32), (((1,), (1,)), ((), ())), preferred_element_type=jnp.float32)
    cell_rates = rate_table[cell_wells]
    inject = lax.dot_general(cell_rates.astype(jnp.float32), prof_onehot.astype(jnp.float32), (((1,), (1,)), ((), ())), preferred_element_type=jnp.float32)
    return (rebuilt + TIME_STEP * (rebuilt - rebuilt * rebuilt * rebuilt + inject)).astype(jnp.bfloat16)

def reference(cell_factor, sched_factor, core_matrix, rate_table, cell_well, sched_profile):
    n_cells = cell_factor.shape[0]
    n_sched = sched_factor.shape[0]
    widths = cell_factor.shape[1]
    blocks = n_cells // CELL_DEV
    profiles = rate_table.shape[1]
    prof_onehot = (sched_profile[:, None] == jnp.arange(profiles, dtype=jnp.int32)[None, :]).astype(jnp.bfloat16)
    factor_blocks = cell_factor.reshape(blocks, CELL_DEV, widths)
    well_blocks = cell_well.reshape(blocks, CELL_DEV)

    def first(carry, inputs):
        cell_rows, cell_wells = inputs
        tile_state = build_tile(cell_rows, cell_wells, sched_factor, core_matrix, rate_table, prof_onehot)
        k_part = jnp.dot(tile_state.astype(jnp.float32), sched_factor.astype(jnp.float32), preferred_element_type=jnp.float32)
        l_part = lax.dot_general(tile_state.astype(jnp.float32), cell_rows.astype(jnp.float32), (((0,), (0,)), ((), ())), preferred_element_type=jnp.float32)
        return (carry + l_part, k_part)
    l_proj, k_parts = lax.scan(first, jnp.zeros((n_sched, widths), jnp.float32), (factor_blocks, well_blocks))
    k_proj = k_parts.reshape(n_cells, widths)
    panel_u = jnp.concatenate([cell_factor.astype(jnp.float32), k_proj * (PANEL_SCALE / n_sched)], axis=1)
    panel_v = jnp.concatenate([sched_factor.astype(jnp.float32), l_proj * (PANEL_SCALE / n_cells)], axis=1)
    basis_u = orthonormal(panel_u)
    basis_v = orthonormal(panel_v)
    basis_low = basis_v.astype(jnp.bfloat16)
    basis_blocks = basis_u.reshape(blocks, CELL_DEV, 2 * widths)

    def second(carry, inputs):
        cell_rows, cell_wells, basis_rows = inputs
        tile_state = build_tile(cell_rows, cell_wells, sched_factor, core_matrix, rate_table, prof_onehot)
        galerkin = jnp.dot(tile_state.astype(jnp.float32), basis_low.astype(jnp.float32), preferred_element_type=jnp.float32)
        term = lax.dot_general(basis_rows, galerkin, (((0,), (0,)), ((), ())), precision=lax.Precision.HIGHEST)
        return (carry + term, 0)
    core_sum, unused = lax.scan(second, jnp.zeros((2 * widths, 2 * widths), jnp.float32), (factor_blocks, well_blocks, basis_blocks))
    basis_cells = basis_u * jnp.sqrt(jnp.float32(n_cells))
    basis_sched = basis_v * jnp.sqrt(jnp.float32(n_sched))
    core_out = core_sum * (widths / jnp.sqrt(jnp.float32(n_cells) * jnp.float32(n_sched)))
    return (basis_cells, basis_sched, core_out)
```

```python
import jax
import jax.numpy as jnp
from jax import lax
from jax.sharding import PartitionSpec as P

TIME_STEP = 0.25
PANEL_SCALE = 8.0
HI = lax.Precision.HIGHEST
f32, bf16 = jnp.float32, jnp.bfloat16


def dot(a, b, ca, cb, precision=None):
    return lax.dot_general(
        a, b, (((ca,), (cb,)), ((), ())), precision=precision, preferred_element_type=f32
    )


def swap(x, bit, n):
    return lax.ppermute(x, "cell", [(i, i ^ (1 << bit)) for i in range(n)])


def all_sum(x, n):
    me = lax.axis_index("cell")
    bits = n.bit_length() - 1
    half = x.shape[0] // 2
    odd = (me & 1) == 1
    lo, hi = x[:half], x[half:]
    mine = jnp.where(odd, hi, lo) + swap(jnp.where(odd, lo, hi), 0, n)
    for bit in range(1, bits):
        mine = mine + swap(mine, bit, n)
    other = swap(mine, 0, n)
    return jnp.concatenate([jnp.where(odd, other, mine), jnp.where(odd, mine, other)], axis=0)


def scatter_sum(x, order, n):
    bits = len(order)
    x = x.reshape((2,) * bits + x.shape[1:])
    left = list(range(bits - 1, -1, -1))
    for bit in order:
        ax = left.index(bit)
        send = lax.index_in_dim(x, 1, ax, keepdims=False).astype(bf16)
        keep = lax.index_in_dim(x, 0, ax, keepdims=False)
        x = keep + swap(send, bit, n).astype(f32)
        left.pop(ax)
    return x


def chol_inv(gram):
    low = jnp.linalg.cholesky(gram)
    eye = jnp.eye(gram.shape[0], dtype=f32)
    inv = lax.linalg.triangular_solve(low, eye, left_side=True, lower=True)
    return low, inv


def local(cell_factor, sched_factor, core_matrix, rate_table, cell_well, sched_profile):
    cells_dev, rank = cell_factor.shape
    n_sched = sched_factor.shape[0]
    n = lax.axis_size("cell")
    n_cells = cells_dev * n
    wells, profiles = rate_table.shape
    me = lax.axis_index("cell")
    blk = n_sched // n
    ck = PANEL_SCALE / n_sched
    cl = PANEL_SCALE / n_cells
    C = cell_factor
    S = jnp.concatenate(
        [lax.dynamic_slice_in_dim(sched_factor, (me ^ p) * blk, blk, 0) for p in range(n)], axis=0
    )
    prof = jnp.concatenate(
        [lax.dynamic_slice_in_dim(sched_profile, (me ^ p) * blk, blk, 0) for p in range(n)], axis=0
    )
    F = jnp.dot(C.astype(f32), core_matrix, precision=HI).astype(bf16)
    W = (cell_well[:, None] == jnp.arange(wells, dtype=jnp.int32)[None, :]).astype(bf16)
    R = jnp.dot(W, rate_table, preferred_element_type=f32).astype(bf16)
    Pt = (jnp.arange(profiles, dtype=jnp.int32)[:, None] == prof[None, :]).astype(bf16)
    r = dot(F, S, 1, 1)
    G = ((1.0 + TIME_STEP) * r - TIME_STEP * (r * r * r)).astype(bf16)
    PS = dot(Pt, S, 1, 0)
    k = (dot(G, S, 1, 0) + TIME_STEP * dot(R.astype(f32), PS, 1, 0, HI)) * ck
    Cf = C.astype(f32)
    CC = dot(C, C, 0, 0)
    Ck = dot(Cf, k, 0, 0, HI)
    kk = dot(k, k, 0, 0, HI)
    sums = all_sum(jnp.concatenate([CC, Ck, kk], axis=0), n)
    CC, Ck, kk = sums[:rank], sums[rank : 2 * rank], sums[2 * rank :]

    def inj(lhs, lhs_t_g):
        A = TIME_STEP * dot(lhs, R, 0, 0)
        hi = A.astype(bf16)
        lo = (A - hi.astype(f32)).astype(bf16)
        return lhs_t_g + dot(hi, Pt, 1, 0) + dot(lo, Pt, 1, 0)

    kb = k.astype(bf16)
    lt = inj(C, dot(C, G, 0, 0)) * cl
    m2 = inj(kb, dot(kb, G, 0, 0))
    bits = n.bit_length() - 1
    order_a = list(range(bits))
    order_b = [0] + [2, 1] + list(range(3, bits)) if bits > 2 else order_a
    lt = scatter_sum(lt.reshape(rank, n, blk).transpose(1, 0, 2), order_a, n)
    m2 = scatter_sum(m2.reshape(rank, n, blk).transpose(1, 0, 2), order_b, n)
    ll = dot(lt, lt, 1, 1, HI)
    n22 = dot(m2, lt, 1, 1, HI)
    sums = all_sum(jnp.concatenate([ll, n22], axis=0), n)
    ll, n22 = sums[:rank], sums[rank:]

    L11u, A = chol_inv(CC)
    L21u = dot(Ck, A, 0, 1, HI)
    L22u, D = chol_inv(kk - dot(L21u, L21u, 1, 1, HI))
    Xu = dot(A, L21u, 0, 1, HI)
    root_c = jnp.sqrt(jnp.float32(n_cells))
    u1 = dot(Cf, A, 1, 1, HI) * root_c
    u2 = dot(k - dot(Cf, Xu, 1, 0, HI), D, 1, 1, HI) * root_c
    basis_cells = jnp.concatenate([u1, u2], axis=1)
    SS = dot(sched_factor, sched_factor, 0, 0)
    L11v, Av = chol_inv(SS)
    L21v = dot(Ck * (cl / ck), Av, 1, 1, HI)
    L22v, Dv = chol_inv(ll - dot(L21v, L21v, 1, 1, HI))
    Xv = dot(Av, L21v, 0, 1, HI)
    root_s = jnp.sqrt(jnp.float32(n_sched))
    own = S[:blk].astype(f32)
    v1 = dot(own, Av, 1, 1, HI) * root_s
    v2 = dot(lt.T - dot(own, Xv, 1, 0, HI), Dv, 1, 1, HI) * root_s
    basis_sched = jnp.concatenate([v1, v2], axis=1)
    scale = rank / jnp.sqrt(jnp.float32(n_cells) * jnp.float32(n_sched))
    B = -dot(dot(D, L21u, 1, 0, HI), A, 1, 0, HI)
    c11 = dot(A, L21v, 1, 0, HI) / cl
    c12 = dot(A, L22v, 1, 0, HI) / cl
    c21 = dot(L22u, Av, 0, 1, HI) / ck
    E = dot(B, ll, 1, 0, HI) / cl + dot(D, n22, 1, 0, HI) - dot(L22u, Xv, 0, 0, HI) / ck
    c22 = dot(E, Dv, 1, 1, HI)
    core_out = (
        jnp.concatenate(
            [jnp.concatenate([c11, c12], axis=1), jnp.concatenate([c21, c22], axis=1)], axis=0
        )
        * scale
    )
    return (basis_cells, basis_sched, core_out)


def solution(mesh):
    return jax.shard_map(
        local,
        mesh=mesh,
        in_specs=(
            P(("group", "cell"), None),
            P("group", None),
            P("group", None),
            P(),
            P(("group", "cell")),
            P("group"),
        ),
        out_specs=(P(("group", "cell"), None), P(("group", "cell"), None), P("group", None)),
        check_vma=False,
    )
```

```python
import jax
import jax.numpy as jnp
from jax import lax
from jax.experimental import pallas as pl
from jax.experimental.pallas import tpu as pltpu
from jax.sharding import PartitionSpec as P

TIME_STEP = 0.25
PANEL_SCALE = 8.0
HI = lax.Precision.HIGHEST
f32, bf16, i32 = jnp.float32, jnp.bfloat16, jnp.int32


def dot(a, b, ca, cb, precision=None):
    return lax.dot_general(
        a, b, (((ca,), (cb,)), ((), ())), precision=precision, preferred_element_type=f32
    )


def split(x):
    hi = x.astype(bf16)
    return hi, (x - hi.astype(f32)).astype(bf16)


def swap(x, bit, n):
    return lax.ppermute(x, "cell", [(i, i ^ (1 << bit)) for i in range(n)])


def all_sum(x, n):
    me = lax.axis_index("cell")
    bits = n.bit_length() - 1
    half = x.shape[0] // 2
    odd = (me & 1) == 1
    lo, hi = x[:half], x[half:]
    mine = jnp.where(odd, hi, lo) + swap(jnp.where(odd, lo, hi), 0, n)
    for bit in range(1, bits):
        mine = mine + swap(mine, bit, n)
    other = swap(mine, 0, n)
    return jnp.concatenate([jnp.where(odd, other, mine), jnp.where(odd, mine, other)], axis=0)


def scatter_sum(send, keep, order, n):
    x = keep.astype(f32) + swap(send, order[0], n).astype(f32)
    for bit in order[1:]:
        half = x.shape[0] // 2
        x = x[:half] + swap(x[half:].astype(bf16), bit, n).astype(f32)
    return x[0]


def state_kernel(ck, cl, chunk, perm_ref, slot_ref, c_ref, s_ref, core_ref, table_ref, well_ref,
                 prof_ref, k_ref, gram_ref, ls_ref, lk_ref, ms_ref, mk_ref,
                 g_ref, f_ref, ps_ref, ckt_ref, inj_ref):
    n, blk, rank = s_ref.shape
    cells = c_ref.shape[0]
    wells, profiles = table_ref.shape
    c = c_ref[...]
    core = core_ref[...]
    c1, rest = core.astype(bf16), core - core.astype(bf16).astype(f32)
    c2, c3 = split(rest)
    f_ref[...] = (dot(c, c1, 1, 0) + dot(c, c2, 1, 0) + dot(c, c3, 1, 0)).astype(bf16)
    k_ref[...] = jnp.zeros_like(k_ref)
    ps_ref[...] = jnp.zeros_like(ps_ref)

    def onehot(b):
        ids = lax.broadcasted_iota(i32, (profiles, blk), 0)
        return jnp.where(ids == prof_ref[b], 1.0, 0.0).astype(bf16)

    def first(j, carry):
        b = perm_ref[j]
        s = s_ref[b]
        for t in range(cells // chunk):
            rows = pl.ds(t * chunk, chunk)
            r = dot(f_ref[rows, :], s, 1, 1)
            g = (r * ((1.0 + TIME_STEP) - TIME_STEP * (r * r))).astype(bf16)
            g_ref[j, rows, :] = g
            k_ref[rows, :] += dot(g, s, 1, 0)
        ps_ref[...] += dot(onehot(b), s, 1, 0)
        return carry

    lax.fori_loop(0, n, first, 0)

    table = table_ref[...]
    wt = jnp.where(
        lax.broadcasted_iota(i32, (wells, cells), 0) == well_ref[...], 1.0, 0.0
    ).astype(bf16)
    ps_hi, ps_lo = split(ps_ref[...])
    tp_hi, tp_lo = split(dot(table, ps_hi, 1, 0) + dot(table, ps_lo, 1, 0))
    k = (k_ref[...] + TIME_STEP * (dot(wt, tp_hi, 0, 0) + dot(wt, tp_lo, 0, 0))) * ck
    k_ref[...] = k
    ct = c.astype(f32).T.astype(bf16)
    kt_hi, kt_lo = split(k.T)
    k_hi, k_lo = split(k)
    ckt_ref[:rank, :] = ct
    ckt_ref[rank:, :] = kt_hi
    gram_ref[:rank, :] = dot(ct, c, 1, 0)
    gram_ref[rank : 2 * rank, :] = dot(ct, k_hi, 1, 0) + dot(ct, k_lo, 1, 0)
    gram_ref[2 * rank :, :] = dot(kt_hi, k_hi, 1, 0) + (dot(kt_hi, k_lo, 1, 0) + dot(kt_lo, k_hi, 1, 0))
    w_hi, w_lo = split(dot(ckt_ref[...], wt, 1, 1))
    a_hi, a_lo = split(TIME_STEP * (dot(w_hi, table, 1, 0) + dot(w_lo, table, 1, 0)))
    inj_ref[:, :profiles] = a_hi
    inj_ref[:, profiles:] = a_lo

    def block(j):
        hot = onehot(perm_ref[j])
        out = dot(ckt_ref[...], g_ref[j], 1, 0) + dot(
            inj_ref[...], jnp.concatenate([hot, hot], axis=0), 1, 0
        )
        return (out[:rank] * cl).astype(bf16), out[rank:].astype(bf16)

    half = n // 2

    def second_keep(j, carry):
        lk_ref[j], mk_ref[slot_ref[j]] = block(j)
        return carry

    def second_send(j, carry):
        ls_ref[j], ms_ref[slot_ref[j]] = block(half + j)
        return carry

    lax.fori_loop(0, half, second_send, 0)
    lax.fori_loop(0, half, second_keep, 0)


def eliminate(w_refs):
    m = w_refs[0].shape[0]
    for p in range(m // 8):
        base = 8 * p
        for w in w_refs:
            rows = [jnp.broadcast_to(w[base + i : base + i + 1, :], (8, 2 * m)) for i in range(8)]
            cell = [
                [jnp.broadcast_to(rows[r][:, base + i : base + i + 1], (8, m)) for i in range(r + 1)]
                for r in range(8)
            ]
            for i in range(8):
                inv = lax.rsqrt(cell[i][i])
                inv2 = jnp.concatenate([inv, inv], axis=1)
                rows[i] = rows[i] * inv2
                mult = [None] * 8
                for r in range(i + 1, 8):
                    mult[r] = cell[r][i] * inv
                for r in range(i + 1, 8):
                    for q in range(i + 1, r + 1):
                        cell[r][q] = cell[r][q] - mult[r] * mult[q]
                    rows[r] = rows[r] - jnp.concatenate([mult[r], mult[r]], axis=1) * rows[i]
            for i in range(8):
                w[base + i : base + i + 1, :] = rows[i][:1, :]
            if base + 8 < m:
                u = w[base : base + 8, :]
                w[base + 8 :, :] -= dot(u[:, base + 8 : m], u, 0, 0, HI)


def load_gram(w, gram):
    m = gram.shape[0]
    row = lax.broadcasted_iota(i32, (m, m), 0)
    col = lax.broadcasted_iota(i32, (m, m), 1)
    w[:, :m] = gram
    w[:, m:] = jnp.where(row == col, 1.0, 0.0)


def upper(w):
    m = w.shape[0]
    row = lax.broadcasted_iota(i32, (m, m), 0)
    col = lax.broadcasted_iota(i32, (m, m), 1)
    return jnp.where(col >= row, w[:, :m], 0.0), jnp.where(col <= row, w[:, m:], 0.0)


def lead_kernel(ratio, gram_ref, ss_ref, lead_ref, wu, wv):
    m = ss_ref.shape[0]
    load_gram(wu, gram_ref[:m, :])
    load_gram(wv, ss_ref[...])
    eliminate([wu, wv])
    a, av = upper(wu)[1], upper(wv)[1]
    ck = gram_ref[m : 2 * m, :]
    l21u = dot(ck, a, 0, 1, HI)
    l21v = dot(ck * ratio, av, 1, 1, HI)
    lead_ref[0] = a
    lead_ref[1] = l21u
    lead_ref[2] = dot(a, l21u, 0, 1, HI)
    lead_ref[3] = gram_ref[2 * m :, :] - dot(l21u, l21u, 1, 1, HI)
    lead_ref[4] = av
    lead_ref[5] = l21v
    lead_ref[6] = dot(av, l21v, 0, 1, HI)
    lead_ref[7] = dot(l21v, l21v, 1, 1, HI)


def cells_kernel(root, lead_ref, c_ref, k_ref, basis_ref, lt_ref, inv_ref, w):
    m = w.shape[0]
    load_gram(w, lead_ref[3])
    eliminate([w])
    lt, d = upper(w)
    lt_ref[...] = lt
    inv_ref[...] = d
    c = c_ref[...].astype(f32)
    basis_ref[:, :m] = dot(c, lead_ref[0], 1, 1, HI) * root
    basis_ref[:, m:] = dot(k_ref[...] - dot(c, lead_ref[2], 1, 0, HI), d, 1, 1, HI) * root


def plans_kernel(root, ck, cl, scale, sums_ref, lead_ref, ltu_ref, d_ref, s_ref, l_ref,
                 basis_ref, core_ref, w):
    m = w.shape[0]
    ll = sums_ref[:m, :]
    n22 = sums_ref[m:, :]
    load_gram(w, ll - lead_ref[7])
    eliminate([w])
    ltv, dv = upper(w)
    a, l21u, av, l21v, xv = (lead_ref[i] for i in (0, 1, 4, 5, 6))
    d = d_ref[...]
    own = s_ref[...].astype(f32)
    basis_ref[:, :m] = dot(own, av, 1, 1, HI) * root
    basis_ref[:, m:] = dot(l_ref[...].T - dot(own, xv, 1, 0, HI), dv, 1, 1, HI) * root
    b = -dot(dot(d, l21u, 1, 0, HI), a, 1, 0, HI)
    e = dot(b, ll, 1, 0, HI) * (1.0 / cl) + dot(d, n22, 1, 0, HI) - dot(ltu_ref[...], xv, 1, 0, HI) * (1.0 / ck)
    core_ref[:m, :m] = dot(a, l21v, 1, 0, HI) * (scale / cl)
    core_ref[:m, m:] = dot(a, ltv, 1, 1, HI) * (scale / cl)
    core_ref[m:, :m] = dot(ltu_ref[...], av, 1, 1, HI) * (scale / ck)
    core_ref[m:, m:] = dot(e, dv, 1, 1, HI) * scale


def params(mib):
    return pltpu.CompilerParams(vmem_limit_bytes=mib << 20)


def local(cell_factor, sched_factor, core_matrix, rate_table, cell_well, sched_profile):
    cells_dev, rank = cell_factor.shape
    n_sched = sched_factor.shape[0]
    n = lax.axis_size("cell")
    n_cells = cells_dev * n
    profiles = rate_table.shape[1]
    me = lax.axis_index("cell")
    blk = n_sched // n
    bits = n.bit_length() - 1
    half = n // 2
    ck = PANEL_SCALE / n_sched
    cl = PANEL_SCALE / n_cells
    order_a = list(range(bits))
    order_b = [0, 2, 1] + order_a[3:] if bits > 2 else order_a
    rel = [sum(((j >> (bits - 1 - i)) & 1) << bit for i, bit in enumerate(order_a)) for j in range(n)]
    slots = [
        sum(((p >> bit) & 1) << (bits - 1 - i) for i, bit in enumerate(order_b)) % half for p in rel[:half]
    ]
    perm = jnp.array(rel, i32) ^ me
    vmem = pl.BlockSpec(memory_space=pltpu.VMEM)
    smem = pl.BlockSpec(memory_space=pltpu.SMEM)
    part = jax.ShapeDtypeStruct((half, rank, blk), bf16)
    k, gram, ls, lk, ms, mk = pl.pallas_call(
        lambda *refs: state_kernel(ck, cl, min(256, cells_dev), *refs),
        out_shape=(
            jax.ShapeDtypeStruct((cells_dev, rank), f32),
            jax.ShapeDtypeStruct((3 * rank, rank), f32),
            part, part, part, part,
        ),
        in_specs=[smem, smem] + [vmem] * 6,
        out_specs=(vmem,) * 6,
        scratch_shapes=[
            pltpu.VMEM((n, cells_dev, blk), bf16),
            pltpu.VMEM((cells_dev, rank), bf16),
            pltpu.VMEM((profiles, rank), f32),
            pltpu.VMEM((2 * rank, cells_dev), bf16),
            pltpu.VMEM((2 * rank, 2 * profiles), bf16),
        ],
        compiler_params=params(48),
        name="state",
    )(
        perm, jnp.array(slots, i32), cell_factor, sched_factor.reshape(n, blk, rank), core_matrix,
        rate_table, cell_well.reshape(1, cells_dev), sched_profile.reshape(n, 1, blk),
    )
    sums = all_sum(gram, n)
    lt = scatter_sum(ls, lk, order_a, n)
    m2 = scatter_sum(ms, mk, order_b, n)
    sums2 = all_sum(jnp.concatenate([dot(lt, lt, 1, 1, HI), dot(m2, lt, 1, 1, HI)], axis=0), n)
    ss = dot(sched_factor, sched_factor, 0, 0)
    pair = pltpu.VMEM((rank, 2 * rank), f32)
    square = jax.ShapeDtypeStruct((rank, rank), f32)
    lead = pl.pallas_call(
        lambda *refs: lead_kernel(cl / ck, *refs),
        out_shape=jax.ShapeDtypeStruct((8, rank, rank), f32),
        in_specs=[vmem] * 2, out_specs=vmem, scratch_shapes=[pair, pair],
        compiler_params=params(16), name="lead",
    )(sums, ss)
    basis_cells, ltu, d = pl.pallas_call(
        lambda *refs: cells_kernel(float(n_cells) ** 0.5, *refs),
        out_shape=(jax.ShapeDtypeStruct((cells_dev, 2 * rank), f32), square, square),
        in_specs=[vmem] * 3, out_specs=(vmem,) * 3, scratch_shapes=[pair],
        compiler_params=params(16), name="cells",
    )(lead, cell_factor, k)
    own = lax.dynamic_slice_in_dim(sched_factor, me * blk, blk, 0)
    scale = rank / (float(n_cells) * float(n_sched)) ** 0.5
    basis_sched, core_out = pl.pallas_call(
        lambda *refs: plans_kernel(float(n_sched) ** 0.5, ck, cl, scale, *refs),
        out_shape=(
            jax.ShapeDtypeStruct((blk, 2 * rank), f32),
            jax.ShapeDtypeStruct((2 * rank, 2 * rank), f32),
        ),
        in_specs=[vmem] * 6, out_specs=(vmem,) * 2, scratch_shapes=[pair],
        compiler_params=params(16), name="plans",
    )(sums2, lead, ltu, d, own, lt)
    return (basis_cells, basis_sched, core_out)


def solution(mesh):
    return jax.shard_map(
        local,
        mesh=mesh,
        in_specs=(
            P(("group", "cell"), None),
            P("group", None),
            P("group", None),
            P(),
            P(("group", "cell")),
            P("group"),
        ),
        out_specs=(P(("group", "cell"), None), P(("group", "cell"), None), P("group", None)),
        check_vma=False,
    )
```

```python
import jax
import jax.numpy as jnp
from jax import lax
from jax.experimental import pallas as pl
from jax.experimental.pallas import tpu as pltpu
from jax.sharding import PartitionSpec as P

TIME_STEP = 0.25
PANEL_SCALE = 8.0
HI = lax.Precision.HIGHEST
f32, bf16, i32 = jnp.float32, jnp.bfloat16, jnp.int32


def dot(a, b, ca, cb, precision=None):
    return lax.dot_general(
        a, b, (((ca,), (cb,)), ((), ())), precision=precision, preferred_element_type=f32
    )


def split(x):
    hi = x.astype(bf16)
    return hi, (x - hi.astype(f32)).astype(bf16)


def swap(x, mask, n):
    return lax.ppermute(x, "cell", [(i, i ^ mask) for i in range(n)])


def all_sum(x, n):
    me = lax.axis_index("cell")
    bits = n.bit_length() - 1
    half = x.shape[0] // 2
    odd = (me & 1) == 1
    lo, hi = x[:half], x[half:]
    mine = jnp.where(odd, hi, lo) + swap(jnp.where(odd, lo, hi), 1, n)
    for bit in range(1, bits):
        mine = mine + swap(mine, 1 << bit, n)
    other = swap(mine, 1, n)
    return jnp.concatenate([jnp.where(odd, other, mine), jnp.where(odd, mine, other)], axis=0)


def state_kernel(ck, cl, block_ref, slot_ref, c_hbm, s_hbm, core_hbm, table_hbm, well_hbm, prof_hbm,
                 k_ref, gram_ref, send_l, send_m, hold_l, hold_m,
                 c_ref, s_ref, core_ref, table_ref, well_ref, prof_ref,
                 g_ref, ft_ref, ps_ref, kt_ref, both_ref, inj_ref, l_ref, m_ref, sems, out_sems):
    n, blk, rank = s_ref.shape
    cells = c_ref.shape[0]
    half = n // 2
    wells, profiles = table_ref.shape
    copies = [
        pltpu.make_async_copy(src, dst, sems.at[i])
        for i, (src, dst) in enumerate(
            [(c_hbm, c_ref), (core_hbm, core_ref), (s_hbm, s_ref), (prof_hbm, prof_ref),
             (table_hbm, table_ref), (well_hbm, well_ref)]
        )
    ]
    for copy in copies:
        copy.start()
    kt_ref[...] = jnp.zeros_like(kt_ref)
    ps_ref[...] = jnp.zeros_like(ps_ref)
    copies[0].wait()
    copies[1].wait()
    c = c_ref[...]
    core = core_ref[...]
    c1 = core.astype(bf16)
    c2, c3 = split(core - c1.astype(f32))
    ft_ref[...] = (dot(c, c1, 1, 0) + dot(c, c2, 1, 0) + dot(c, c3, 1, 0)).T.astype(bf16)
    for copy in copies[2:]:
        copy.wait()

    def first(b, carry):
        s = s_ref[b]
        r = dot(s, ft_ref[...], 1, 0)
        g = (r * ((1.0 + TIME_STEP) - TIME_STEP * (r * r))).astype(bf16)
        g_ref[b] = g
        kt_ref[...] += dot(s, g, 0, 0)
        ps_ref[...] += dot(onehot(prof_ref[b], profiles, blk), s, 1, 0)
        return carry

    lax.fori_loop(0, n, first, 0, unroll=2)

    table = table_ref[...]
    wt = onehot(well_ref[...], wells, cells)
    ps_hi, ps_lo = split(ps_ref[...])
    tp_hi, tp_lo = split(dot(table, ps_hi, 1, 0) + dot(table, ps_lo, 1, 0))
    kt = (kt_ref[...] + TIME_STEP * (dot(tp_hi, wt, 0, 0) + dot(tp_lo, wt, 0, 0))) * ck
    k = kt.T
    k_ref[...] = k
    ct = c.astype(f32).T.astype(bf16)
    kt_hi, kt_lo = split(kt)
    k_hi, k_lo = split(k)
    both_ref[:, :rank] = c
    both_ref[:, rank:] = k_hi
    w_hi, w_lo = split(dot(wt, both_ref[...], 1, 0))
    a_hi, a_lo = split(TIME_STEP * (dot(table, w_hi, 0, 0) + dot(table, w_lo, 0, 0)))
    inj_ref[:profiles, :] = a_hi
    inj_ref[profiles:, :] = a_lo
    gram_ref[:rank, :] = dot(ct, c, 1, 0)
    gram_ref[rank : 2 * rank, :] = dot(ct, k_hi, 1, 0) + dot(ct, k_lo, 1, 0)
    gram_ref[2 * rank :, :] = dot(kt_hi, k_hi, 1, 0) + (dot(kt_hi, k_lo, 1, 0) + dot(kt_lo, k_hi, 1, 0))

    def outgoing(j, at, dst_l, dst_m):
        return (
            pltpu.make_async_copy(l_ref.at[j], dst_l.at[at], out_sems.at[0, j]),
            pltpu.make_async_copy(m_ref.at[j], dst_m.at[slot_ref[at]], out_sems.at[1, j]),
        )

    def second(first_slot, dst_l, dst_m):
        def body(at, carry):
            j = first_slot + at
            b = block_ref[j]
            hot = onehot(prof_ref[b], profiles, blk)
            out = dot(g_ref[b], both_ref[...], 1, 0) + dot(
                jnp.concatenate([hot, hot], axis=0), inj_ref[...], 0, 0
            )
            l_ref[j] = (out[:, :rank] * cl).astype(bf16)
            m_ref[j] = out[:, rank:].astype(bf16)
            for copy in outgoing(j, at, dst_l, dst_m):
                copy.start()
            return carry

        lax.fori_loop(0, half, body, 0)

    def finish(first_slot, dst_l, dst_m):
        def body(at, carry):
            for copy in outgoing(first_slot + at, at, dst_l, dst_m):
                copy.wait()
            return carry

        lax.fori_loop(0, half, body, 0)

    second(half, send_l, send_m)
    second(0, hold_l, hold_m)
    finish(half, send_l, send_m)
    finish(0, hold_l, hold_m)


def onehot(ids, size, count):
    return jnp.where(lax.broadcasted_iota(i32, (size, count), 0) == ids, 1.0, 0.0).astype(bf16)


def fold_kernel(keep_l, came_l, keep_m, came_m, after, send_l, hold_l, send_m, hold_m):
    half = hold_l.shape[0]
    for keep, came, send, hold in ((keep_l, came_l, send_l, hold_l), (keep_m, came_m, send_m, hold_m)):
        for j in range(half):
            hold[j] = (keep[j].astype(f32) + came[j].astype(f32)).astype(bf16)
            send[j] = (keep[half + j].astype(f32) + came[half + j].astype(f32)).astype(bf16)


def pair_kernel(keep_l, came_l, keep_m, came_m, after, l_ref, sums_ref):
    rank = l_ref.shape[1]
    l = keep_l[0].astype(f32) + came_l[0].astype(f32)
    m2 = keep_m[0].astype(f32) + came_m[0].astype(f32)
    l_ref[...] = l
    sums_ref[:rank, :] = dot(l, l, 0, 0, HI)
    sums_ref[rank:, :] = dot(m2, l, 0, 0, HI)


def spread(row, col, m):
    return jnp.broadcast_to(row[:, col : col + 1], (8, m))


def eliminate(w_refs):
    m = w_refs[0].shape[0]

    def take(w, base):
        left = [jnp.broadcast_to(w[base + i : base + i + 1, :m], (8, m)) for i in range(8)]
        right = [jnp.broadcast_to(w[base + i : base + i + 1, m:], (8, m)) for i in range(8)]
        cell = [[spread(left[r], base + i, m) for i in range(r + 1)] for r in range(8)]
        return left, right, cell

    held = [take(w, 0) for w in w_refs]
    for base in range(0, m, 8):
        after = base + 8
        for at, w in enumerate(w_refs):
            left, right, cell = held[at]
            if after < m:
                next_left, next_right, next_cell = take(w, after)
            for i in range(8):
                inv = lax.rsqrt(cell[i][i])
                left[i] = left[i] * inv
                right[i] = right[i] * inv
                mult = [None] * 8
                for r in range(i + 1, 8):
                    mult[r] = cell[r][i] * inv
                for r in range(i + 1, 8):
                    for q in range(i + 1, r + 1):
                        cell[r][q] = cell[r][q] - mult[r] * mult[q]
                    left[r] = left[r] - mult[r] * left[i]
                    right[r] = right[r] - mult[r] * right[i]
                w[base + i : base + i + 1, :m] = left[i][:1, :]
                w[base + i : base + i + 1, m:] = right[i][:1, :]
                if after < m:
                    ahead = [spread(left[i], after + r, m) for r in range(8)]
                    for r in range(8):
                        for q in range(r + 1):
                            next_cell[r][q] = next_cell[r][q] - ahead[r] * ahead[q]
                        next_left[r] = next_left[r] - ahead[r] * left[i]
                        next_right[r] = next_right[r] - ahead[r] * right[i]
            if after + 8 < m:
                u = w[base:after, :]
                w[after + 8 :, :] -= dot(u[:, after + 8 : m], u, 0, 0, HI)
            if after < m:
                held[at] = (next_left, next_right, next_cell)


def load_gram(w, gram):
    m = gram.shape[0]
    row = lax.broadcasted_iota(i32, (m, m), 0)
    col = lax.broadcasted_iota(i32, (m, m), 1)
    w[:, :m] = gram
    w[:, m:] = jnp.where(row == col, 1.0, 0.0)


def upper(w):
    m = w.shape[0]
    row = lax.broadcasted_iota(i32, (m, m), 0)
    col = lax.broadcasted_iota(i32, (m, m), 1)
    return jnp.where(col >= row, w[:, :m], 0.0), jnp.where(col <= row, w[:, m:], 0.0)


def plans_lead_kernel(ss_ref, av_ref, w):
    load_gram(w, ss_ref[...])
    eliminate([w])
    av_ref[...] = upper(w)[1]


def lead_kernel(ratio, gram_ref, av_ref, lead_ref, w):
    m = av_ref.shape[0]
    load_gram(w, gram_ref[:m, :])
    av = av_ref[...]
    ck = gram_ref[m : 2 * m, :]
    l21v = dot(ck * ratio, av, 1, 1, HI)
    lead_ref[4] = av
    lead_ref[5] = l21v
    lead_ref[6] = dot(av, l21v, 0, 1, HI)
    lead_ref[7] = dot(l21v, l21v, 1, 1, HI)
    eliminate([w])
    a = upper(w)[1]
    l21u = dot(ck, a, 0, 1, HI)
    lead_ref[0] = a
    lead_ref[1] = l21u
    lead_ref[2] = dot(a, l21u, 0, 1, HI)
    lead_ref[3] = gram_ref[2 * m :, :] - dot(l21u, l21u, 1, 1, HI)


def cells_kernel(root, lead_ref, c_ref, k_ref, basis_ref, lt_ref, inv_ref, w):
    m = w.shape[0]
    load_gram(w, lead_ref[3])
    eliminate([w])
    lt, d = upper(w)
    lt_ref[...] = lt
    inv_ref[...] = d
    c = c_ref[...].astype(f32)
    basis_ref[:, :m] = dot(c, lead_ref[0], 1, 1, HI) * root
    basis_ref[:, m:] = dot(k_ref[...] - dot(c, lead_ref[2], 1, 0, HI), d, 1, 1, HI) * root


def plans_kernel(root, ck, cl, scale, sums_ref, lead_ref, ltu_ref, d_ref, s_ref, l_ref,
                 basis_ref, core_ref, w):
    m = w.shape[0]
    ll = sums_ref[:m, :]
    n22 = sums_ref[m:, :]
    load_gram(w, ll - lead_ref[7])
    eliminate([w])
    ltv, dv = upper(w)
    a, l21u, av, l21v, xv = (lead_ref[i] for i in (0, 1, 4, 5, 6))
    d = d_ref[...]
    own = s_ref[...].astype(f32)
    basis_ref[:, :m] = dot(own, av, 1, 1, HI) * root
    basis_ref[:, m:] = dot(l_ref[...] - dot(own, xv, 1, 0, HI), dv, 1, 1, HI) * root
    b = -dot(dot(d, l21u, 1, 0, HI), a, 1, 0, HI)
    e = dot(b, ll, 1, 0, HI) * (1.0 / cl) + dot(d, n22, 1, 0, HI) - dot(ltu_ref[...], xv, 1, 0, HI) * (1.0 / ck)
    core_ref[:m, :m] = dot(a, l21v, 1, 0, HI) * (scale / cl)
    core_ref[:m, m:] = dot(a, ltv, 1, 1, HI) * (scale / cl)
    core_ref[m:, :m] = dot(ltu_ref[...], av, 1, 1, HI) * (scale / ck)
    core_ref[m:, m:] = dot(e, dv, 1, 1, HI) * scale


def params(mib):
    return pltpu.CompilerParams(vmem_limit_bytes=mib << 20)


def local(cell_factor, sched_factor, core_matrix, rate_table, cell_well, sched_profile):
    cells_dev, rank = cell_factor.shape
    n_sched = sched_factor.shape[0]
    n = lax.axis_size("cell")
    n_cells = cells_dev * n
    profiles = rate_table.shape[1]
    me = lax.axis_index("cell")
    blk = n_sched // n
    bits = n.bit_length() - 1
    half = n // 2
    ck = PANEL_SCALE / n_sched
    cl = PANEL_SCALE / n_cells
    order_a = list(range(bits))
    order_b = [0, 2, 1] + order_a[3:] if bits > 2 else order_a
    rel = [sum(((j >> (bits - 1 - i)) & 1) << bit for i, bit in enumerate(order_a)) for j in range(n)]
    slots = [
        sum(((p >> bit) & 1) << (bits - 1 - i) for i, bit in enumerate(order_b)) % half for p in rel[:half]
    ]
    perm = jnp.array(rel, i32) ^ me
    vmem = pl.BlockSpec(memory_space=pltpu.VMEM)
    smem = pl.BlockSpec(memory_space=pltpu.SMEM)
    hbm = pl.BlockSpec(memory_space=pltpu.HBM)
    anywhere = pl.BlockSpec(memory_space=pl.ANY)

    def shape(dtype, *dims):
        return jax.ShapeDtypeStruct(dims, dtype)

    part = shape(bf16, half, blk, rank)
    k, gram, send_l, send_m, hold_l, hold_m = pl.pallas_call(
        lambda *refs: state_kernel(ck, cl, *refs),
        out_shape=(shape(f32, cells_dev, rank), shape(f32, 3 * rank, rank), part, part, part, part),
        in_specs=[smem] * 2 + [hbm] * 6,
        out_specs=(vmem,) * 2 + (hbm,) * 4,
        scratch_shapes=[
            pltpu.VMEM((cells_dev, rank), bf16),
            pltpu.VMEM((n, blk, rank), bf16),
            pltpu.VMEM((rank, rank), f32),
            pltpu.VMEM(rate_table.shape, bf16),
            pltpu.VMEM((1, cells_dev), i32),
            pltpu.VMEM((n, 1, blk), i32),
            pltpu.VMEM((n, blk, cells_dev), bf16),
            pltpu.VMEM((rank, cells_dev), bf16),
            pltpu.VMEM((profiles, rank), f32),
            pltpu.VMEM((rank, cells_dev), f32),
            pltpu.VMEM((cells_dev, 2 * rank), bf16),
            pltpu.VMEM((2 * profiles, 2 * rank), bf16),
            pltpu.VMEM((n, blk, rank), bf16),
            pltpu.VMEM((n, blk, rank), bf16),
            pltpu.SemaphoreType.DMA((6,)),
            pltpu.SemaphoreType.DMA((2, n)),
        ],
        compiler_params=params(60),
        name="state",
    )(
        perm, jnp.array(slots, i32), cell_factor, sched_factor.reshape(n, blk, rank), core_matrix,
        rate_table, cell_well.reshape(1, cells_dev), sched_profile.reshape(n, 1, blk),
    )
    sums = all_sum(gram, n)
    ss = dot(sched_factor, sched_factor, 0, 0)
    pair = pltpu.VMEM((rank, 2 * rank), f32)
    square = jax.ShapeDtypeStruct((rank, rank), f32)
    av = pl.pallas_call(
        plans_lead_kernel, out_shape=square, in_specs=[vmem], out_specs=vmem, scratch_shapes=[pair],
        compiler_params=params(16), name="plans_lead",
    )(ss)
    lead = pl.pallas_call(
        lambda *refs: lead_kernel(cl / ck, *refs),
        out_shape=jax.ShapeDtypeStruct((8, rank, rank), f32),
        in_specs=[vmem] * 2, out_specs=vmem, scratch_shapes=[pair],
        compiler_params=params(16), name="lead",
    )(sums, av)
    basis_cells, ltu, d = pl.pallas_call(
        lambda *refs: cells_kernel(float(n_cells) ** 0.5, *refs),
        out_shape=(shape(f32, cells_dev, 2 * rank), square, square),
        in_specs=[vmem] * 3, out_specs=(vmem,) * 3, scratch_shapes=[pair],
        compiler_params=params(16), name="cells",
    )(lead, cell_factor, k)
    waits = [gram, av] + [lead] * (bits - 3) + [d]
    for step in range(bits):
        came_l = swap(send_l, 1 << order_a[step], n)
        came_m = swap(send_m, 1 << order_b[step], n)
        args = (hold_l, came_l, hold_m, came_m, waits[step])
        specs = [vmem] * 4 + [anywhere]
        if step < bits - 1:
            part = shape(bf16, half >> (step + 1), blk, rank)
            send_l, hold_l, send_m, hold_m = pl.pallas_call(
                fold_kernel, out_shape=(part,) * 4, in_specs=specs, out_specs=(vmem,) * 4,
                compiler_params=params(16), name="fold",
            )(*args)
        else:
            lt, sums2 = pl.pallas_call(
                pair_kernel, out_shape=(shape(f32, blk, rank), shape(f32, 2 * rank, rank)),
                in_specs=specs, out_specs=(vmem,) * 2, compiler_params=params(16), name="pair",
            )(*args)
    sums2 = all_sum(sums2, n)
    own = lax.dynamic_slice_in_dim(sched_factor, me * blk, blk, 0)
    scale = rank / (float(n_cells) * float(n_sched)) ** 0.5
    basis_sched, core_out = pl.pallas_call(
        lambda *refs: plans_kernel(float(n_sched) ** 0.5, ck, cl, scale, *refs),
        out_shape=(
            jax.ShapeDtypeStruct((blk, 2 * rank), f32),
            jax.ShapeDtypeStruct((2 * rank, 2 * rank), f32),
        ),
        in_specs=[vmem] * 6, out_specs=(vmem,) * 2, scratch_shapes=[pair],
        compiler_params=params(16), name="plans",
    )(sums2, lead, ltu, d, own, lt)
    return (basis_cells, basis_sched, core_out)


def solution(mesh):
    return jax.shard_map(
        local,
        mesh=mesh,
        in_specs=(
            P(("group", "cell"), None),
            P("group", None),
            P("group", None),
            P(),
            P(("group", "cell")),
            P("group"),
        ),
        out_specs=(P(("group", "cell"), None), P(("group", "cell"), None), P("group", None)),
        check_vma=False,
    )
```

```python
import jax
import jax.numpy as jnp
from jax import lax
from jax.experimental import pallas as pl
from jax.experimental.pallas import tpu as pltpu
from jax.sharding import PartitionSpec as P

TIME_STEP = 0.25
PANEL_SCALE = 8.0
HI = lax.Precision.HIGHEST
f32, bf16, i32 = jnp.float32, jnp.bfloat16, jnp.int32


def dot(a, b, ca, cb, precision=None):
    return lax.dot_general(
        a, b, (((ca,), (cb,)), ((), ())), precision=precision, preferred_element_type=f32
    )


def split(x):
    hi = x.astype(bf16)
    return hi, (x - hi.astype(f32)).astype(bf16)


def swap(x, mask, n):
    return lax.ppermute(x, "cell", [(i, i ^ mask) for i in range(n)])


def diagonal(m):
    return lax.broadcasted_iota(i32, (m, m), 0) - lax.broadcasted_iota(i32, (m, m), 1)


def cut(rows_ref, send_ref, keep_ref):
    half = send_ref.shape[0]
    odd = lax.rem(lax.axis_index("cell"), 2)
    send_ref[...] = rows_ref[pl.ds(pl.multiple_of((1 - odd) * half, 8), half), :]
    keep_ref[...] = rows_ref[pl.ds(pl.multiple_of(odd * half, 8), half), :]


def joined(rows_ref, mine_ref, other_ref):
    half = mine_ref.shape[0]
    odd = lax.rem(lax.axis_index("cell"), 2)
    rows_ref[pl.ds(pl.multiple_of(odd * half, 8), half), :] = mine_ref[...]
    rows_ref[pl.ds(pl.multiple_of((1 - odd) * half, 8), half), :] = other_ref[...]


def state_kernel(ck, cl, relative, slot_of, c_hbm, s_hbm, core_hbm, table_hbm, well_hbm, prof_hbm,
                 k_ref, gsend_ref, gkeep_ref, send_l, send_m, hold_l, hold_m,
                 c_ref, s_ref, core_ref, table_ref, well_ref, prof_ref,
                 g_ref, ft_ref, ps_ref, kt_ref, both_ref, inj_ref, l_ref, m_ref, gram_ref, sems, out_sems):
    n, blk, rank = s_ref.shape
    cells = c_ref.shape[0]
    half = n // 2
    wells, profiles = table_ref.shape
    copies = [
        pltpu.make_async_copy(src, dst, sems.at[i])
        for i, (src, dst) in enumerate(
            [(c_hbm, c_ref), (core_hbm, core_ref), (s_hbm, s_ref), (prof_hbm, prof_ref),
             (table_hbm, table_ref), (well_hbm, well_ref)]
        )
    ]
    for copy in copies:
        copy.start()
    kt_ref[...] = jnp.zeros_like(kt_ref)
    ps_ref[...] = jnp.zeros_like(ps_ref)
    copies[0].wait()
    copies[1].wait()
    c = c_ref[...]
    core = core_ref[...]
    c1 = core.astype(bf16)
    c2, c3 = split(core - c1.astype(f32))
    ft_ref[...] = (dot(c, c1, 1, 0) + dot(c, c2, 1, 0) + dot(c, c3, 1, 0)).T.astype(bf16)
    for copy in copies[2:]:
        copy.wait()

    def first(b, carry):
        s = s_ref[b]
        r = dot(s, ft_ref[...], 1, 0)
        g = (r * ((1.0 + TIME_STEP) - TIME_STEP * (r * r))).astype(bf16)
        g_ref[b] = g
        kt_ref[...] += dot(s, g, 0, 0)
        ps_ref[...] += dot(onehot(prof_ref[b], profiles, blk), s, 1, 0)
        return carry

    lax.fori_loop(0, n, first, 0, unroll=2)

    table = table_ref[...]
    wt = onehot(well_ref[...], wells, cells)
    ps_hi, ps_lo = split(ps_ref[...])
    tp_hi, tp_lo = split(dot(table, ps_hi, 1, 0) + dot(table, ps_lo, 1, 0))
    kt = (kt_ref[...] + TIME_STEP * (dot(tp_hi, wt, 0, 0) + dot(tp_lo, wt, 0, 0))) * ck
    k = kt.T
    k_ref[...] = k
    ct = c.astype(f32).T.astype(bf16)
    kt_hi, kt_lo = split(kt)
    k_hi, k_lo = split(k)
    both_ref[:, :rank] = c
    both_ref[:, rank:] = k_hi
    w_hi, w_lo = split(dot(wt, both_ref[...], 1, 0))
    a_hi, a_lo = split(TIME_STEP * (dot(table, w_hi, 0, 0) + dot(table, w_lo, 0, 0)))
    inj_ref[:profiles, :] = a_hi
    inj_ref[profiles:, :] = a_lo
    cc = dot(ct, c, 1, 0)
    kk = dot(kt_hi, k_hi, 1, 0) + (dot(kt_hi, k_lo, 1, 0) + dot(kt_lo, k_hi, 1, 0))
    below = diagonal(rank)
    gram_ref[:rank, :] = dot(ct, k_hi, 1, 0) + dot(ct, k_lo, 1, 0)
    gram_ref[rank : 2 * rank, :] = jnp.where(below > 0, cc, kk)
    gram_ref[2 * rank :, :] = jnp.broadcast_to(
        jnp.sum(jnp.where(below == 0, cc, 0.0), axis=0, keepdims=True), (16, rank)
    )
    cut(gram_ref, gsend_ref, gkeep_ref)
    me = lax.axis_index("cell")

    def outgoing(j, at, dst_l, dst_m):
        return (
            pltpu.make_async_copy(l_ref.at[j], dst_l.at[at], out_sems.at[0, j]),
            pltpu.make_async_copy(m_ref.at[j], dst_m.at[slot_of(at)], out_sems.at[1, j]),
        )

    def second(first_slot, dst_l, dst_m):
        def body(at, carry):
            j = first_slot + at
            b = me ^ relative(j)
            hot = onehot(prof_ref[b], profiles, blk)
            out = dot(g_ref[b], both_ref[...], 1, 0) + dot(
                jnp.concatenate([hot, hot], axis=0), inj_ref[...], 0, 0
            )
            l_ref[j] = (out[:, :rank] * cl).astype(bf16)
            m_ref[j] = out[:, rank:].astype(bf16)
            for copy in outgoing(j, at, dst_l, dst_m):
                copy.start()
            return carry

        lax.fori_loop(0, half, body, 0)

    def finish(first_slot, dst_l, dst_m):
        def body(at, carry):
            for copy in outgoing(first_slot + at, at, dst_l, dst_m):
                copy.wait()
            return carry

        lax.fori_loop(0, half, body, 0)

    second(half, send_l, send_m)
    second(0, hold_l, hold_m)
    finish(half, send_l, send_m)
    finish(0, hold_l, hold_m)


def onehot(ids, size, count):
    return jnp.where(lax.broadcasted_iota(i32, (size, count), 0) == ids, 1.0, 0.0).astype(bf16)


def fold_kernel(keep_l, came_l, keep_m, came_m, after, send_l, hold_l, send_m, hold_m):
    half = hold_l.shape[0]
    for keep, came, send, hold in ((keep_l, came_l, send_l, hold_l), (keep_m, came_m, send_m, hold_m)):
        for j in range(half):
            hold[j] = (keep[j].astype(f32) + came[j].astype(f32)).astype(bf16)
            send[j] = (keep[half + j].astype(f32) + came[half + j].astype(f32)).astype(bf16)


def first_fold_kernel(keep_l0, keep_l1, came_l0, came_l1, keep_m0, keep_m1, came_m0, came_m1, after,
                      send_l, hold_l, send_m, hold_m):
    for keep, came, out in (
        (keep_l0, came_l0, hold_l), (keep_l1, came_l1, send_l),
        (keep_m0, came_m0, hold_m), (keep_m1, came_m1, send_m),
    ):
        out[...] = (keep[...].astype(f32) + came[...].astype(f32)).astype(bf16)


def pair_kernel(keep_l, came_l, keep_m, came_m, after, l_ref, send_ref, keep_ref, sums_ref):
    rank = l_ref.shape[1]
    l = keep_l[0].astype(f32) + came_l[0].astype(f32)
    m2 = keep_m[0].astype(f32) + came_m[0].astype(f32)
    l_ref[...] = l
    sums_ref[:rank, :] = dot(l, l, 0, 0, HI)
    sums_ref[rank:, :] = dot(m2, l, 0, 0, HI)
    cut(sums_ref, send_ref, keep_ref)


def spread(row, col, m):
    return jnp.broadcast_to(row[:, col : col + 1], (8, m))


def eliminate(w_refs):
    m = w_refs[0].shape[0]

    def take(w, base):
        left = [jnp.broadcast_to(w[base + i : base + i + 1, :m], (8, m)) for i in range(8)]
        right = [jnp.broadcast_to(w[base + i : base + i + 1, m:], (8, m)) for i in range(8)]
        cell = [[spread(left[r], base + i, m) for i in range(r + 1)] for r in range(8)]
        return left, right, cell

    held = [take(w, 0) for w in w_refs]
    for base in range(0, m, 8):
        after = base + 8
        for at, w in enumerate(w_refs):
            left, right, cell = held[at]
            if after < m:
                next_left, next_right, next_cell = take(w, after)
            for i in range(8):
                inv = lax.rsqrt(cell[i][i])
                left[i] = left[i] * inv
                right[i] = right[i] * inv
                mult = [None] * 8
                for r in range(i + 1, 8):
                    mult[r] = cell[r][i] * inv
                for r in range(i + 1, 8):
                    for q in range(i + 1, r + 1):
                        cell[r][q] = cell[r][q] - mult[r] * mult[q]
                    left[r] = left[r] - mult[r] * left[i]
                    right[r] = right[r] - mult[r] * right[i]
                w[base + i : base + i + 1, :m] = left[i][:1, :]
                w[base + i : base + i + 1, m:] = right[i][:1, :]
                if after < m:
                    ahead = [spread(left[i], after + r, m) for r in range(8)]
                    for r in range(8):
                        for q in range(r + 1):
                            next_cell[r][q] = next_cell[r][q] - ahead[r] * ahead[q]
                        next_left[r] = next_left[r] - ahead[r] * left[i]
                        next_right[r] = next_right[r] - ahead[r] * right[i]
            if after + 8 < m:
                u = w[base:after, :]
                w[after + 8 :, :] -= dot(u[:, after + 8 : m], u, 0, 0, HI)
            if after < m:
                held[at] = (next_left, next_right, next_cell)


def load_gram(w, gram):
    m = gram.shape[0]
    row = lax.broadcasted_iota(i32, (m, m), 0)
    col = lax.broadcasted_iota(i32, (m, m), 1)
    w[:, :m] = gram
    w[:, m:] = jnp.where(row == col, 1.0, 0.0)


def upper(w):
    m = w.shape[0]
    row = lax.broadcasted_iota(i32, (m, m), 0)
    col = lax.broadcasted_iota(i32, (m, m), 1)
    return jnp.where(col >= row, w[:, :m], 0.0), jnp.where(col <= row, w[:, m:], 0.0)


def plans_lead_kernel(ss_ref, after, av_ref, w):
    load_gram(w, ss_ref[...])
    eliminate([w])
    av_ref[...] = upper(w)[1]


def lead_kernel(ratio, mine_ref, other_ref, av_ref, after, lead_ref, w, gram_ref):
    m = av_ref.shape[0]
    joined(gram_ref, mine_ref, other_ref)
    below = diagonal(m)
    mixed = gram_ref[m : 2 * m, :]
    low = jnp.where(below > 0, mixed, 0.0)
    high = jnp.where(below <= 0, mixed, 0.0)
    strict = jnp.where(below < 0, mixed, 0.0)
    load_gram(w, low + low.T + jnp.where(below == 0, gram_ref[2 * m : 2 * m + 1, :], 0.0))
    av = av_ref[...]
    ck = gram_ref[:m, :]
    l21v = dot(ck * ratio, av, 1, 1, HI)
    lead_ref[4] = av
    lead_ref[5] = l21v
    lead_ref[6] = dot(av, l21v, 0, 1, HI)
    lead_ref[7] = dot(l21v, l21v, 1, 1, HI)
    eliminate([w])
    a = upper(w)[1]
    l21u = dot(ck, a, 0, 1, HI)
    lead_ref[0] = a
    lead_ref[1] = l21u
    lead_ref[2] = dot(a, l21u, 0, 1, HI)
    lead_ref[3] = high + strict.T - dot(l21u, l21u, 1, 1, HI)


def cells_kernel(root, lead_ref, c_ref, k_ref, basis_ref, lt_ref, inv_ref, w):
    m = w.shape[0]
    load_gram(w, lead_ref[3])
    eliminate([w])
    lt, d = upper(w)
    lt_ref[...] = lt
    inv_ref[...] = d
    c = c_ref[...].astype(f32)
    basis_ref[:, :m] = dot(c, lead_ref[0], 1, 1, HI) * root
    basis_ref[:, m:] = dot(k_ref[...] - dot(c, lead_ref[2], 1, 0, HI), d, 1, 1, HI) * root


def plans_kernel(root, ck, cl, scale, mine_ref, other_ref, lead_ref, ltu_ref, d_ref, s_ref, l_ref,
                 basis_ref, core_ref, w, sums_ref):
    m = w.shape[0]
    joined(sums_ref, mine_ref, other_ref)
    ll = sums_ref[:m, :]
    n22 = sums_ref[m:, :]
    load_gram(w, ll - lead_ref[7])
    eliminate([w])
    ltv, dv = upper(w)
    a, l21u, av, l21v, xv = (lead_ref[i] for i in (0, 1, 4, 5, 6))
    d = d_ref[...]
    own = s_ref[...].astype(f32)
    basis_ref[:, :m] = dot(own, av, 1, 1, HI) * root
    basis_ref[:, m:] = dot(l_ref[...] - dot(own, xv, 1, 0, HI), dv, 1, 1, HI) * root
    b = -dot(dot(d, l21u, 1, 0, HI), a, 1, 0, HI)
    e = dot(b, ll, 1, 0, HI) * (1.0 / cl) + dot(d, n22, 1, 0, HI) - dot(ltu_ref[...], xv, 1, 0, HI) * (1.0 / ck)
    core_ref[:m, :m] = dot(a, l21v, 1, 0, HI) * (scale / cl)
    core_ref[:m, m:] = dot(a, ltv, 1, 1, HI) * (scale / cl)
    core_ref[m:, :m] = dot(ltu_ref[...], av, 1, 1, HI) * (scale / ck)
    core_ref[m:, m:] = dot(e, dv, 1, 1, HI) * scale


def params(mib):
    return pltpu.CompilerParams(vmem_limit_bytes=mib << 20)


def local(cell_factor, sched_factor, core_matrix, rate_table, cell_well, sched_profile):
    cells_dev, rank = cell_factor.shape
    n_sched = sched_factor.shape[0]
    n = lax.axis_size("cell")
    n_cells = cells_dev * n
    profiles = rate_table.shape[1]
    me = lax.axis_index("cell")
    blk = n_sched // n
    bits = n.bit_length() - 1
    half = n // 2
    ck = PANEL_SCALE / n_sched
    cl = PANEL_SCALE / n_cells
    order_a = list(range(bits))
    order_b = [0, 2, 1] + order_a[3:] if bits > 2 else order_a

    def relative(j):
        return sum(((j >> (bits - 1 - i)) & 1) << bit for i, bit in enumerate(order_a))

    def slot_of(at):
        p = relative(at)
        return sum(((p >> bit) & 1) << (bits - 1 - i) for i, bit in enumerate(order_b) if i > 0)

    vmem = pl.BlockSpec(memory_space=pltpu.VMEM)
    hbm = pl.BlockSpec(memory_space=pltpu.HBM)
    anywhere = pl.BlockSpec(memory_space=pl.ANY)

    def shape(dtype, *dims):
        return jax.ShapeDtypeStruct(dims, dtype)

    part = shape(bf16, half, blk, rank)
    gram_half = shape(f32, rank + 8, rank)
    k, gram_send, gram, send_l, send_m, hold_l, hold_m = pl.pallas_call(
        lambda *refs: state_kernel(ck, cl, relative, slot_of, *refs),
        out_shape=(shape(f32, cells_dev, rank), gram_half, gram_half, part, part, part, part),
        in_specs=[hbm] * 6,
        out_specs=(vmem,) * 3 + (hbm,) * 4,
        scratch_shapes=[
            pltpu.VMEM((cells_dev, rank), bf16),
            pltpu.VMEM((n, blk, rank), bf16),
            pltpu.VMEM((rank, rank), f32),
            pltpu.VMEM(rate_table.shape, bf16),
            pltpu.VMEM((1, cells_dev), i32),
            pltpu.VMEM((n, 1, blk), i32),
            pltpu.VMEM((n, blk, cells_dev), bf16),
            pltpu.VMEM((rank, cells_dev), bf16),
            pltpu.VMEM((profiles, rank), f32),
            pltpu.VMEM((rank, cells_dev), f32),
            pltpu.VMEM((cells_dev, 2 * rank), bf16),
            pltpu.VMEM((2 * profiles, 2 * rank), bf16),
            pltpu.VMEM((n, blk, rank), bf16),
            pltpu.VMEM((n, blk, rank), bf16),
            pltpu.VMEM((2 * rank + 16, rank), f32),
            pltpu.SemaphoreType.DMA((6,)),
            pltpu.SemaphoreType.DMA((2, n)),
        ],
        compiler_params=params(60),
        name="state",
    )(
        cell_factor, sched_factor.reshape(n, blk, rank), core_matrix,
        rate_table, cell_well.reshape(1, cells_dev), sched_profile.reshape(n, 1, blk),
    )
    ss = dot(sched_factor, sched_factor, 0, 0)
    pair = pltpu.VMEM((rank, 2 * rank), f32)
    square = shape(f32, rank, rank)

    came_l, came_m = swap(send_l, 1, n), swap(send_m, 1, n)
    gram = gram + swap(gram_send, 1, n)
    quarter = half // 2
    block = (1, blk, rank)
    near = pl.BlockSpec(block, lambda j: (j, 0, 0))
    far = pl.BlockSpec(block, lambda j: (quarter + j, 0, 0))
    part = shape(bf16, quarter, blk, rank)
    send_l, hold_l, send_m, hold_m = pl.pallas_call(
        first_fold_kernel, grid=(quarter,), out_shape=(part,) * 4,
        in_specs=[near, far] * 4 + [anywhere], out_specs=(near,) * 4, compiler_params=params(20), name="first_fold",
    )(hold_l, hold_l, came_l, came_l, hold_m, hold_m, came_m, came_m, gram)

    def fold(step, send_l, hold_l, send_m, hold_m, came_l, came_m, after):
        part = shape(bf16, half >> (step + 1), blk, rank)
        return pl.pallas_call(
            fold_kernel, out_shape=(part,) * 4, in_specs=[vmem] * 4 + [anywhere], out_specs=(vmem,) * 4,
            compiler_params=params(16), name="fold",
        )(hold_l, came_l, hold_m, came_m, after)

    gram = gram + swap(gram, 1 << order_a[1], n)
    came_l, came_m = swap(send_l, 1 << order_a[1], n), swap(send_m, 1 << order_b[1], n)
    gram_came = swap(gram, 1 << order_a[2], n)
    av = pl.pallas_call(
        plans_lead_kernel, out_shape=square, in_specs=[vmem, anywhere], out_specs=vmem,
        scratch_shapes=[pair], compiler_params=params(16), name="plans_lead",
    )(ss, gram)
    send_l, hold_l, send_m, hold_m = fold(1, send_l, hold_l, send_m, hold_m, came_l, came_m, av)
    gram = gram + gram_came
    for bit in range(3, bits):
        gram = gram + swap(gram, 1 << bit, n)
    gram_other = swap(gram, 1, n)
    for step in range(2, bits - 1):
        came_l = swap(send_l, 1 << order_a[step], n)
        came_m = swap(send_m, 1 << order_b[step], n)
        send_l, hold_l, send_m, hold_m = fold(step, send_l, hold_l, send_m, hold_m, came_l, came_m, gram_other)
    came_l, came_m = swap(send_l, 1 << order_a[-1], n), swap(send_m, 1 << order_b[-1], n)
    lead = pl.pallas_call(
        lambda *refs: lead_kernel(cl / ck, *refs),
        out_shape=shape(f32, 8, rank, rank),
        in_specs=[vmem] * 3 + [anywhere], out_specs=vmem,
        scratch_shapes=[pair, pltpu.VMEM((2 * rank + 16, rank), f32)],
        compiler_params=params(16), name="lead",
    )(gram, gram_other, av, hold_l)
    basis_cells, ltu, d = pl.pallas_call(
        lambda *refs: cells_kernel(float(n_cells) ** 0.5, *refs),
        out_shape=(shape(f32, cells_dev, 2 * rank), square, square),
        in_specs=[vmem] * 3, out_specs=(vmem,) * 3, scratch_shapes=[pair],
        compiler_params=params(16), name="cells",
    )(lead, cell_factor, k)
    lt, sums_send, sums = pl.pallas_call(
        pair_kernel, out_shape=(shape(f32, blk, rank), square, square),
        in_specs=[vmem] * 4 + [anywhere], out_specs=(vmem,) * 3,
        scratch_shapes=[pltpu.VMEM((2 * rank, rank), f32)],
        compiler_params=params(16), name="pair",
    )(hold_l, came_l, hold_m, came_m, d)
    sums = sums + swap(sums_send, 1, n)
    for bit in range(1, bits):
        sums = sums + swap(sums, 1 << bit, n)
    sums_other = swap(sums, 1, n)
    own = lax.dynamic_slice_in_dim(sched_factor, me * blk, blk, 0)
    scale = rank / (float(n_cells) * float(n_sched)) ** 0.5
    basis_sched, core_out = pl.pallas_call(
        lambda *refs: plans_kernel(float(n_sched) ** 0.5, ck, cl, scale, *refs),
        out_shape=(
            jax.ShapeDtypeStruct((blk, 2 * rank), f32),
            jax.ShapeDtypeStruct((2 * rank, 2 * rank), f32),
        ),
        in_specs=[vmem] * 7, out_specs=(vmem,) * 2,
        scratch_shapes=[pair, pltpu.VMEM((2 * rank, rank), f32)],
        compiler_params=params(16), name="plans",
    )(sums, sums_other, lead, ltu, d, own, lt)
    return (basis_cells, basis_sched, core_out)


def solution(mesh):
    return jax.shard_map(
        local,
        mesh=mesh,
        in_specs=(
            P(("group", "cell"), None),
            P("group", None),
            P("group", None),
            P(),
            P(("group", "cell")),
            P("group"),
        ),
        out_specs=(P(("group", "cell"), None), P(("group", "cell"), None), P("group", None)),
        check_vma=False,
    )
```

```python
import jax
import jax.numpy as jnp
from jax import lax
from jax.experimental import pallas as pl
from jax.experimental.pallas import tpu as pltpu
from jax.sharding import PartitionSpec as P

TIME_STEP = 0.25
PANEL_SCALE = 8.0
HI = lax.Precision.HIGHEST
f32, bf16, i32 = jnp.float32, jnp.bfloat16, jnp.int32


def dot(a, b, ca, cb, precision=None):
    return lax.dot_general(
        a, b, (((ca,), (cb,)), ((), ())), precision=precision, preferred_element_type=f32
    )


def split(x):
    hi = x.astype(bf16)
    return hi, (x - hi.astype(f32)).astype(bf16)


def swap(x, mask, n):
    return lax.ppermute(x, "cell", [(i, i ^ mask) for i in range(n)])


def diagonal(m):
    return lax.broadcasted_iota(i32, (m, m), 0) - lax.broadcasted_iota(i32, (m, m), 1)


def cut(rows_ref, send_ref, keep_ref):
    half = send_ref.shape[0]
    odd = lax.rem(lax.axis_index("cell"), 2)
    send_ref[...] = rows_ref[pl.ds(pl.multiple_of((1 - odd) * half, 8), half), :]
    keep_ref[...] = rows_ref[pl.ds(pl.multiple_of(odd * half, 8), half), :]


def joined(rows_ref, mine_ref, other_ref):
    half = mine_ref.shape[0]
    odd = lax.rem(lax.axis_index("cell"), 2)
    rows_ref[pl.ds(pl.multiple_of(odd * half, 8), half), :] = mine_ref[...]
    rows_ref[pl.ds(pl.multiple_of((1 - odd) * half, 8), half), :] = other_ref[...]


def state_kernel(ck, cl, relative, slot_of, c_hbm, s_hbm, core_hbm, table_hbm, well_hbm, prof_hbm,
                 k_ref, gsend_ref, gkeep_ref, send_l, send_m, hold_l, hold_m,
                 c_ref, s_ref, core_ref, table_ref, well_ref, prof_ref,
                 g_ref, ft_ref, ps_ref, kt_ref, both_ref, inj_ref, l_ref, m_ref, gram_ref, sems, out_sems):
    n, blk, rank = s_ref.shape
    cells = c_ref.shape[0]
    half = n // 2
    wells, profiles = table_ref.shape
    copies = [
        pltpu.make_async_copy(src, dst, sems.at[i])
        for i, (src, dst) in enumerate(
            [(c_hbm, c_ref), (core_hbm, core_ref), (s_hbm, s_ref), (prof_hbm, prof_ref),
             (table_hbm, table_ref), (well_hbm, well_ref)]
        )
    ]
    for copy in copies:
        copy.start()
    kt_ref[...] = jnp.zeros_like(kt_ref)
    ps_ref[...] = jnp.zeros_like(ps_ref)
    copies[0].wait()
    copies[1].wait()
    c = c_ref[...]
    core = core_ref[...]
    c1 = core.astype(bf16)
    c2, c3 = split(core - c1.astype(f32))
    ft_ref[...] = (dot(c, c1, 1, 0) + dot(c, c2, 1, 0) + dot(c, c3, 1, 0)).T.astype(bf16)
    for copy in copies[2:]:
        copy.wait()

    def first(b, carry):
        s = s_ref[b]
        r = dot(s, ft_ref[...], 1, 0)
        g = (r * ((1.0 + TIME_STEP) - TIME_STEP * (r * r))).astype(bf16)
        g_ref[b] = g
        kt_ref[...] += dot(s, g, 0, 0)
        ps_ref[...] += dot(onehot(prof_ref[b], profiles, blk), s, 1, 0)
        return carry

    lax.fori_loop(0, n, first, 0, unroll=2)

    table = table_ref[...]
    wt = onehot(well_ref[...], wells, cells)
    ps_hi, ps_lo = split(ps_ref[...])
    tp_hi, tp_lo = split(dot(table, ps_hi, 1, 0) + dot(table, ps_lo, 1, 0))
    kt = (kt_ref[...] + TIME_STEP * (dot(tp_hi, wt, 0, 0) + dot(tp_lo, wt, 0, 0))) * ck
    k = kt.T
    k_ref[...] = k
    ct = c.astype(f32).T.astype(bf16)
    kt_hi, kt_lo = split(kt)
    k_hi, k_lo = split(k)
    both_ref[:, :rank] = c
    both_ref[:, rank:] = k_hi
    w_hi, w_lo = split(dot(wt, both_ref[...], 1, 0))
    a_hi, a_lo = split(TIME_STEP * (dot(table, w_hi, 0, 0) + dot(table, w_lo, 0, 0)))
    inj_ref[:profiles, :] = a_hi
    inj_ref[profiles:, :] = a_lo
    cc = dot(ct, c, 1, 0)
    kk = dot(kt_hi, k_hi, 1, 0) + (dot(kt_hi, k_lo, 1, 0) + dot(kt_lo, k_hi, 1, 0))
    below = diagonal(rank)
    gram_ref[:rank, :] = dot(ct, k_hi, 1, 0) + dot(ct, k_lo, 1, 0)
    gram_ref[rank : 2 * rank, :] = jnp.where(below > 0, cc, kk)
    gram_ref[2 * rank :, :] = jnp.broadcast_to(
        jnp.sum(jnp.where(below == 0, cc, 0.0), axis=0, keepdims=True), (16, rank)
    )
    cut(gram_ref, gsend_ref, gkeep_ref)
    me = lax.axis_index("cell")

    def outgoing(j, at, dst_l, dst_m):
        return (
            pltpu.make_async_copy(l_ref.at[j], dst_l.at[at], out_sems.at[0, j]),
            pltpu.make_async_copy(m_ref.at[j], dst_m.at[slot_of(at)], out_sems.at[1, j]),
        )

    def second(first_slot, dst_l, dst_m):
        def body(at, carry):
            j = first_slot + at
            b = me ^ relative(j)
            hot = onehot(prof_ref[b], profiles, blk)
            out = dot(g_ref[b], both_ref[...], 1, 0) + dot(
                jnp.concatenate([hot, hot], axis=0), inj_ref[...], 0, 0
            )
            l_ref[j] = (out[:, :rank] * cl).astype(bf16)
            m_ref[j] = out[:, rank:].astype(bf16)
            for copy in outgoing(j, at, dst_l, dst_m):
                copy.start()
            return carry

        lax.fori_loop(0, half, body, 0, unroll=2)

    def finish(first_slot, dst_l, dst_m):
        def body(at, carry):
            for copy in outgoing(first_slot + at, at, dst_l, dst_m):
                copy.wait()
            return carry

        lax.fori_loop(0, half, body, 0)

    second(half, send_l, send_m)
    second(0, hold_l, hold_m)
    finish(half, send_l, send_m)
    finish(0, hold_l, hold_m)


def onehot(ids, size, count):
    return jnp.where(lax.broadcasted_iota(i32, (size, count), 0) == ids, 1.0, 0.0).astype(bf16)


def fold_kernel(keep_l, came_l, keep_m, came_m, *rest):
    send_l, hold_l, send_m, hold_m = rest[-4:]
    half = hold_l.shape[0]
    for keep, came, send, hold in ((keep_l, came_l, send_l, hold_l), (keep_m, came_m, send_m, hold_m)):
        for j in range(half):
            hold[j] = (keep[j].astype(f32) + came[j].astype(f32)).astype(bf16)
            send[j] = (keep[half + j].astype(f32) + came[half + j].astype(f32)).astype(bf16)


def first_fold_kernel(keep_l0, keep_l1, came_l0, came_l1, keep_m0, keep_m1, came_m0, came_m1,
                      gram_kept, gram_came, send_l, hold_l, send_m, hold_m, gram_ref):
    @pl.when(pl.program_id(0) == 0)
    def _():
        gram_ref[...] = gram_kept[...] + gram_came[...]

    for keep, came, out in (
        (keep_l0, came_l0, hold_l), (keep_l1, came_l1, send_l),
        (keep_m0, came_m0, hold_m), (keep_m1, came_m1, send_m),
    ):
        out[...] = (keep[...].astype(f32) + came[...].astype(f32)).astype(bf16)


def pair_kernel(keep_l, came_l, keep_m, came_m, after, l_ref, send_ref, keep_ref, sums_ref):
    rank = l_ref.shape[1]
    l = keep_l[0].astype(f32) + came_l[0].astype(f32)
    m2 = keep_m[0].astype(f32) + came_m[0].astype(f32)
    l_ref[...] = l
    sums_ref[:rank, :] = dot(l, l, 0, 0, HI)
    sums_ref[rank:, :] = dot(m2, l, 0, 0, HI)
    cut(sums_ref, send_ref, keep_ref)


def add_kernel(a_ref, b_ref, after, out_ref):
    out_ref[...] = a_ref[...] + b_ref[...]


def spread(row, col, m):
    return jnp.broadcast_to(row[:, col : col + 1], (8, m))


def eliminate(w_refs):
    m = w_refs[0].shape[0]

    def take(w, base):
        left = [jnp.broadcast_to(w[base + i : base + i + 1, :m], (8, m)) for i in range(8)]
        right = [jnp.broadcast_to(w[base + i : base + i + 1, m:], (8, m)) for i in range(8)]
        cell = [[spread(left[r], base + i, m) for i in range(r + 1)] for r in range(8)]
        return left, right, cell

    held = [take(w, 0) for w in w_refs]
    for base in range(0, m, 8):
        after = base + 8
        for at, w in enumerate(w_refs):
            left, right, cell = held[at]
            if after < m:
                next_left, next_right, next_cell = take(w, after)
            for i in range(8):
                inv = lax.rsqrt(cell[i][i])
                left[i] = left[i] * inv
                right[i] = right[i] * inv
                mult = [None] * 8
                for r in range(i + 1, 8):
                    mult[r] = cell[r][i] * inv
                for r in range(i + 1, 8):
                    for q in range(i + 1, r + 1):
                        cell[r][q] = cell[r][q] - mult[r] * mult[q]
                    left[r] = left[r] - mult[r] * left[i]
                    right[r] = right[r] - mult[r] * right[i]
                w[base + i : base + i + 1, :m] = left[i][:1, :]
                w[base + i : base + i + 1, m:] = right[i][:1, :]
                if after < m:
                    ahead = [spread(left[i], after + r, m) for r in range(8)]
                    for r in range(8):
                        for q in range(r + 1):
                            next_cell[r][q] = next_cell[r][q] - ahead[r] * ahead[q]
                        next_left[r] = next_left[r] - ahead[r] * left[i]
                        next_right[r] = next_right[r] - ahead[r] * right[i]
            if after + 8 < m:
                u = w[base:after, :]
                w[after + 8 :, :] -= dot(u[:, after + 8 : m], u, 0, 0, HI)
            if after < m:
                held[at] = (next_left, next_right, next_cell)


def load_gram(w, gram):
    m = gram.shape[0]
    row = lax.broadcasted_iota(i32, (m, m), 0)
    col = lax.broadcasted_iota(i32, (m, m), 1)
    w[:, :m] = gram
    w[:, m:] = jnp.where(row == col, 1.0, 0.0)


def upper(w):
    m = w.shape[0]
    row = lax.broadcasted_iota(i32, (m, m), 0)
    col = lax.broadcasted_iota(i32, (m, m), 1)
    return jnp.where(col >= row, w[:, :m], 0.0), jnp.where(col <= row, w[:, m:], 0.0)


def plans_lead_kernel(ss_ref, after, av_ref, w):
    load_gram(w, ss_ref[...])
    eliminate([w])
    av_ref[...] = upper(w)[1]


def lead_kernel(ratio, mine_ref, other_ref, av_ref, lead_ref, w, gram_ref):
    m = av_ref.shape[0]
    joined(gram_ref, mine_ref, other_ref)
    below = diagonal(m)
    mixed = gram_ref[m : 2 * m, :]
    low = jnp.where(below > 0, mixed, 0.0)
    high = jnp.where(below <= 0, mixed, 0.0)
    strict = jnp.where(below < 0, mixed, 0.0)
    load_gram(w, low + low.T + jnp.where(below == 0, gram_ref[2 * m : 2 * m + 1, :], 0.0))
    av = av_ref[...]
    ck = gram_ref[:m, :]
    l21v = dot(ck * ratio, av, 1, 1, HI)
    lead_ref[4] = av
    lead_ref[5] = l21v
    lead_ref[6] = dot(av, l21v, 0, 1, HI)
    lead_ref[7] = dot(l21v, l21v, 1, 1, HI)
    eliminate([w])
    a = upper(w)[1]
    l21u = dot(ck, a, 0, 1, HI)
    lead_ref[0] = a
    lead_ref[1] = l21u
    lead_ref[2] = dot(a, l21u, 0, 1, HI)
    lead_ref[3] = high + strict.T - dot(l21u, l21u, 1, 1, HI)


def cells_kernel(root, lead_ref, c_ref, k_ref, basis_ref, lt_ref, inv_ref, w):
    m = w.shape[0]
    load_gram(w, lead_ref[3])
    eliminate([w])
    lt, d = upper(w)
    lt_ref[...] = lt
    inv_ref[...] = d
    c = c_ref[...].astype(f32)
    basis_ref[:, :m] = dot(c, lead_ref[0], 1, 1, HI) * root
    basis_ref[:, m:] = dot(k_ref[...] - dot(c, lead_ref[2], 1, 0, HI), d, 1, 1, HI) * root


def plans_kernel(root, ck, cl, scale, mine_ref, other_ref, lead_ref, ltu_ref, d_ref, s_ref, l_ref,
                 basis_ref, core_ref, w, sums_ref):
    m = w.shape[0]
    joined(sums_ref, mine_ref, other_ref)
    ll = sums_ref[:m, :]
    n22 = sums_ref[m:, :]
    load_gram(w, ll - lead_ref[7])
    eliminate([w])
    ltv, dv = upper(w)
    a, l21u, av, l21v, xv = (lead_ref[i] for i in (0, 1, 4, 5, 6))
    d = d_ref[...]
    own = s_ref[...].astype(f32)
    basis_ref[:, :m] = dot(own, av, 1, 1, HI) * root
    basis_ref[:, m:] = dot(l_ref[...] - dot(own, xv, 1, 0, HI), dv, 1, 1, HI) * root
    b = -dot(dot(d, l21u, 1, 0, HI), a, 1, 0, HI)
    e = dot(b, ll, 1, 0, HI) * (1.0 / cl) + dot(d, n22, 1, 0, HI) - dot(ltu_ref[...], xv, 1, 0, HI) * (1.0 / ck)
    core_ref[:m, :m] = dot(a, l21v, 1, 0, HI) * (scale / cl)
    core_ref[:m, m:] = dot(a, ltv, 1, 1, HI) * (scale / cl)
    core_ref[m:, :m] = dot(ltu_ref[...], av, 1, 1, HI) * (scale / ck)
    core_ref[m:, m:] = dot(e, dv, 1, 1, HI) * scale


def cost(units):
    return pl.CostEstimate(flops=0, bytes_accessed=units * 3_600_000, transcendentals=0)


def params(mib):
    return pltpu.CompilerParams(vmem_limit_bytes=mib << 20)


def local(cell_factor, sched_factor, core_matrix, rate_table, cell_well, sched_profile):
    cells_dev, rank = cell_factor.shape
    n_sched = sched_factor.shape[0]
    n = lax.axis_size("cell")
    n_cells = cells_dev * n
    profiles = rate_table.shape[1]
    me = lax.axis_index("cell")
    blk = n_sched // n
    bits = n.bit_length() - 1
    half = n // 2
    ck = PANEL_SCALE / n_sched
    cl = PANEL_SCALE / n_cells
    order_a = list(range(bits))
    order_b = [0, 2, 1] + order_a[3:] if bits > 2 else order_a

    def relative(j):
        return sum(((j >> (bits - 1 - i)) & 1) << bit for i, bit in enumerate(order_a))

    def slot_of(at):
        p = relative(at)
        return sum(((p >> bit) & 1) << (bits - 1 - i) for i, bit in enumerate(order_b) if i > 0)

    vmem = pl.BlockSpec(memory_space=pltpu.VMEM)
    hbm = pl.BlockSpec(memory_space=pltpu.HBM)
    anywhere = pl.BlockSpec(memory_space=pl.ANY)

    def shape(dtype, *dims):
        return jax.ShapeDtypeStruct(dims, dtype)

    part = shape(bf16, half, blk, rank)
    gram_half = shape(f32, rank + 8, rank)
    k, gram_send, gram, send_l, send_m, hold_l, hold_m = pl.pallas_call(
        lambda *refs: state_kernel(ck, cl, relative, slot_of, *refs),
        out_shape=(shape(f32, cells_dev, rank), gram_half, gram_half, part, part, part, part),
        in_specs=[hbm] * 6,
        out_specs=(vmem,) * 3 + (hbm,) * 4,
        scratch_shapes=[
            pltpu.VMEM((cells_dev, rank), bf16),
            pltpu.VMEM((n, blk, rank), bf16),
            pltpu.VMEM((rank, rank), f32),
            pltpu.VMEM(rate_table.shape, bf16),
            pltpu.VMEM((1, cells_dev), i32),
            pltpu.VMEM((n, 1, blk), i32),
            pltpu.VMEM((n, blk, cells_dev), bf16),
            pltpu.VMEM((rank, cells_dev), bf16),
            pltpu.VMEM((profiles, rank), f32),
            pltpu.VMEM((rank, cells_dev), f32),
            pltpu.VMEM((cells_dev, 2 * rank), bf16),
            pltpu.VMEM((2 * profiles, 2 * rank), bf16),
            pltpu.VMEM((n, blk, rank), bf16),
            pltpu.VMEM((n, blk, rank), bf16),
            pltpu.VMEM((2 * rank + 16, rank), f32),
            pltpu.SemaphoreType.DMA((6,)),
            pltpu.SemaphoreType.DMA((2, n)),
        ],
        compiler_params=params(60),
        name="state",
    )(
        cell_factor, sched_factor.reshape(n, blk, rank), core_matrix,
        rate_table, cell_well.reshape(1, cells_dev), sched_profile.reshape(n, 1, blk),
    )
    ss = dot(sched_factor, sched_factor, 0, 0)
    pair = pltpu.VMEM((rank, 2 * rank), f32)
    square = shape(f32, rank, rank)

    came_l, came_m = swap(send_l, 1, n), swap(send_m, 1, n)
    gram_came = swap(gram_send, 1, n)
    quarter = half // 2
    block = (1, blk, rank)
    near = pl.BlockSpec(block, lambda j: (j, 0, 0))
    far = pl.BlockSpec(block, lambda j: (quarter + j, 0, 0))
    part = shape(bf16, quarter, blk, rank)
    whole = pl.BlockSpec(gram.shape, lambda j: (0, 0))
    send_l, hold_l, send_m, hold_m, gram = pl.pallas_call(
        first_fold_kernel, grid=(quarter,), out_shape=(part,) * 4 + (gram_half,),
        in_specs=[near, far] * 4 + [whole] * 2, out_specs=(near,) * 4 + (whole,), compiler_params=params(20), name="first_fold",
    )(hold_l, hold_l, came_l, came_l, hold_m, hold_m, came_m, came_m, gram, gram_came)

    def fold(step, send_l, hold_l, send_m, hold_m, came_l, came_m, *due):
        part = shape(bf16, half >> (step + 1), blk, rank)
        return pl.pallas_call(
            fold_kernel, out_shape=(part,) * 4, in_specs=[vmem] * 4 + [anywhere] * len(due), out_specs=(vmem,) * 4,
            compiler_params=params(16), name="fold",
        )(hold_l, came_l, hold_m, came_m, *due)

    came_l, came_m = swap(send_l, 1 << order_a[1], n), swap(send_m, 1 << order_b[1], n)
    gram = gram + swap(gram, 1 << order_a[1], n)
    av = pl.pallas_call(
        plans_lead_kernel, out_shape=square, in_specs=[vmem, anywhere], out_specs=vmem,
        scratch_shapes=[pair], compiler_params=params(16), cost_estimate=cost(5), name="plans_lead",
    )(ss, hold_l)
    send_l, hold_l, send_m, hold_m = fold(1, send_l, hold_l, send_m, hold_m, came_l, came_m, av, gram)
    for step in range(2, bits - 1):
        came_l = swap(send_l, 1 << order_a[step], n)
        came_m = swap(send_m, 1 << order_b[step], n)
        gram = gram + swap(gram, 1 << order_a[step], n)
        send_l, hold_l, send_m, hold_m = fold(step, send_l, hold_l, send_m, hold_m, came_l, came_m, gram)
    gram = gram + swap(gram, 1 << order_a[-1], n)
    gram_other = swap(gram, 1, n)
    came_l, came_m = swap(send_l, 1 << order_a[-1], n), swap(send_m, 1 << order_b[-1], n)
    lead = pl.pallas_call(
        lambda *refs: lead_kernel(cl / ck, *refs),
        out_shape=shape(f32, 8, rank, rank),
        in_specs=[vmem] * 3, out_specs=vmem,
        scratch_shapes=[pair, pltpu.VMEM((2 * rank + 16, rank), f32)],
        compiler_params=params(16), cost_estimate=cost(6), name="lead",
    )(gram, gram_other, av)
    basis_cells, ltu, d = pl.pallas_call(
        lambda *refs: cells_kernel(float(n_cells) ** 0.5, *refs),
        out_shape=(shape(f32, cells_dev, 2 * rank), square, square),
        in_specs=[vmem] * 3, out_specs=(vmem,) * 3, scratch_shapes=[pair],
        compiler_params=params(16), cost_estimate=cost(8), name="cells",
    )(lead, cell_factor, k)
    lt, sums_send, sums = pl.pallas_call(
        pair_kernel, out_shape=(shape(f32, blk, rank), square, square),
        in_specs=[vmem] * 4 + [anywhere], out_specs=(vmem,) * 3,
        scratch_shapes=[pltpu.VMEM((2 * rank, rank), f32)],
        compiler_params=params(16), name="pair",
    )(hold_l, came_l, hold_m, came_m, lead)
    sums = sums + swap(sums_send, 1, n)
    for bit in range(1, bits - 1):
        sums = sums + swap(sums, 1 << bit, n)
    sums = pl.pallas_call(
        add_kernel, out_shape=square, in_specs=[vmem] * 2 + [anywhere], out_specs=vmem,
        compiler_params=params(16), name="add",
    )(sums, swap(sums, 1 << (bits - 1), n), d)
    sums_other = swap(sums, 1, n)
    own = lax.dynamic_slice_in_dim(sched_factor, me * blk, blk, 0)
    scale = rank / (float(n_cells) * float(n_sched)) ** 0.5
    basis_sched, core_out = pl.pallas_call(
        lambda *refs: plans_kernel(float(n_sched) ** 0.5, ck, cl, scale, *refs),
        out_shape=(
            jax.ShapeDtypeStruct((blk, 2 * rank), f32),
            jax.ShapeDtypeStruct((2 * rank, 2 * rank), f32),
        ),
        in_specs=[vmem] * 7, out_specs=(vmem,) * 2,
        scratch_shapes=[pair, pltpu.VMEM((2 * rank, rank), f32)],
        compiler_params=params(16), name="plans",
    )(sums, sums_other, lead, ltu, d, own, lt)
    return (basis_cells, basis_sched, core_out)


def solution(mesh):
    return jax.shard_map(
        local,
        mesh=mesh,
        in_specs=(
            P(("group", "cell"), None),
            P("group", None),
            P("group", None),
            P(),
            P(("group", "cell")),
            P("group"),
        ),
        out_specs=(P(("group", "cell"), None), P(("group", "cell"), None), P("group", None)),
        check_vma=False,
    )
```

```python
import jax
import jax.numpy as jnp
from jax import lax
from jax.experimental import pallas as pl
from jax.experimental.pallas import tpu as pltpu
from jax.sharding import PartitionSpec as P

TIME_STEP = 0.25
PANEL_SCALE = 8.0
HI = lax.Precision.HIGHEST
f32, bf16, i32 = jnp.float32, jnp.bfloat16, jnp.int32


def dot(a, b, ca, cb, precision=None):
    return lax.dot_general(
        a, b, (((ca,), (cb,)), ((), ())), precision=precision, preferred_element_type=f32
    )


def split(x):
    hi = x.astype(bf16)
    return hi, (x - hi.astype(f32)).astype(bf16)


def swap(x, mask, n):
    return lax.ppermute(x, "cell", [(i, i ^ mask) for i in range(n)])


def all_sum(x, n):
    parts = lax.all_to_all(x.reshape(n, x.shape[0] // n, x.shape[1]), "cell", 0, 0)
    mine = jnp.sum(parts, axis=0)
    return lax.all_to_all(jnp.broadcast_to(mine, parts.shape), "cell", 0, 0).reshape(x.shape)


def state_kernel(ck, cl, relative, slot_of, c_hbm, s_hbm, core_hbm, table_hbm, well_hbm, prof_hbm,
                 k_ref, gram_ref, send_l, send_m, hold_l, hold_m,
                 c_ref, s_ref, core_ref, table_ref, well_ref, prof_ref,
                 g_ref, ft_ref, ps_ref, kt_ref, both_ref, inj_ref, l_ref, m_ref, sems, out_sems):
    n, blk, rank = s_ref.shape
    cells = c_ref.shape[0]
    half = n // 2
    wells, profiles = table_ref.shape
    copies = [
        pltpu.make_async_copy(src, dst, sems.at[i])
        for i, (src, dst) in enumerate(
            [(c_hbm, c_ref), (core_hbm, core_ref), (s_hbm, s_ref), (prof_hbm, prof_ref),
             (table_hbm, table_ref), (well_hbm, well_ref)]
        )
    ]
    for copy in copies:
        copy.start()
    kt_ref[...] = jnp.zeros_like(kt_ref)
    ps_ref[...] = jnp.zeros_like(ps_ref)
    copies[0].wait()
    copies[1].wait()
    c = c_ref[...]
    core = core_ref[...]
    c1 = core.astype(bf16)
    c2, c3 = split(core - c1.astype(f32))
    ft_ref[...] = (dot(c, c1, 1, 0) + dot(c, c2, 1, 0) + dot(c, c3, 1, 0)).T.astype(bf16)
    for copy in copies[2:]:
        copy.wait()

    def first(b, carry):
        s = s_ref[b]
        r = dot(s, ft_ref[...], 1, 0)
        g = (r * ((1.0 + TIME_STEP) - TIME_STEP * (r * r))).astype(bf16)
        g_ref[b] = g
        kt_ref[...] += dot(s, g, 0, 0)
        ps_ref[...] += dot(onehot(prof_ref[b], profiles, blk), s, 1, 0)
        return carry

    lax.fori_loop(0, n, first, 0, unroll=2)

    table = table_ref[...]
    wt = onehot(well_ref[...], wells, cells)
    ps_hi, ps_lo = split(ps_ref[...])
    tp_hi, tp_lo = split(dot(table, ps_hi, 1, 0) + dot(table, ps_lo, 1, 0))
    kt = (kt_ref[...] + TIME_STEP * (dot(tp_hi, wt, 0, 0) + dot(tp_lo, wt, 0, 0))) * ck
    k = kt.T
    k_ref[...] = k
    ct = c.astype(f32).T.astype(bf16)
    kt_hi, kt_lo = split(kt)
    k_hi, k_lo = split(k)
    both_ref[:, :rank] = c
    both_ref[:, rank:] = k_hi
    w_hi, w_lo = split(dot(wt, both_ref[...], 1, 0))
    a_hi, a_lo = split(TIME_STEP * (dot(table, w_hi, 0, 0) + dot(table, w_lo, 0, 0)))
    inj_ref[:profiles, :] = a_hi
    inj_ref[profiles:, :] = a_lo
    cc = dot(ct, c, 1, 0)
    kk = dot(kt_hi, k_hi, 1, 0) + (dot(kt_hi, k_lo, 1, 0) + dot(kt_lo, k_hi, 1, 0))
    gram_ref[:rank, :] = cc
    gram_ref[rank : 2 * rank, :] = dot(ct, k_hi, 1, 0) + dot(ct, k_lo, 1, 0)
    gram_ref[2 * rank :, :] = kk
    me = lax.axis_index("cell")

    def outgoing(j, at, dst_l, dst_m):
        return (
            pltpu.make_async_copy(l_ref.at[j], dst_l.at[at], out_sems.at[0, j]),
            pltpu.make_async_copy(m_ref.at[j], dst_m.at[slot_of(at)], out_sems.at[1, j]),
        )

    def second(first_slot, dst_l, dst_m):
        def body(at, carry):
            j = first_slot + at
            b = me ^ relative(j)
            hot = onehot(prof_ref[b], profiles, blk)
            out = dot(g_ref[b], both_ref[...], 1, 0) + dot(
                jnp.concatenate([hot, hot], axis=0), inj_ref[...], 0, 0
            )
            l_ref[j] = (out[:, :rank] * cl).astype(bf16)
            m_ref[j] = out[:, rank:].astype(bf16)
            for copy in outgoing(j, at, dst_l, dst_m):
                copy.start()
            return carry

        lax.fori_loop(0, half, body, 0, unroll=2)

    def finish(first_slot, dst_l, dst_m):
        def body(at, carry):
            for copy in outgoing(first_slot + at, at, dst_l, dst_m):
                copy.wait()
            return carry

        lax.fori_loop(0, half, body, 0)

    second(half, send_l, send_m)
    second(0, hold_l, hold_m)
    finish(half, send_l, send_m)
    finish(0, hold_l, hold_m)


def onehot(ids, size, count):
    return jnp.where(lax.broadcasted_iota(i32, (size, count), 0) == ids, 1.0, 0.0).astype(bf16)


def fold_kernel(keep_l, came_l, keep_m, came_m, after, send_l, hold_l, send_m, hold_m):
    half = hold_l.shape[0]
    for keep, came, send, hold in ((keep_l, came_l, send_l, hold_l), (keep_m, came_m, send_m, hold_m)):
        for j in range(half):
            hold[j] = (keep[j].astype(f32) + came[j].astype(f32)).astype(bf16)
            send[j] = (keep[half + j].astype(f32) + came[half + j].astype(f32)).astype(bf16)


def first_fold_kernel(keep_l0, keep_l1, came_l0, came_l1, keep_m0, keep_m1, came_m0, came_m1,
                      send_l, hold_l, send_m, hold_m):
    for keep, came, out in (
        (keep_l0, came_l0, hold_l), (keep_l1, came_l1, send_l),
        (keep_m0, came_m0, hold_m), (keep_m1, came_m1, send_m),
    ):
        out[...] = (keep[...].astype(f32) + came[...].astype(f32)).astype(bf16)


def pair_kernel(keep_l, came_l, keep_m, came_m, after, l_ref, sums_ref):
    rank = l_ref.shape[1]
    l = keep_l[0].astype(f32) + came_l[0].astype(f32)
    m2 = keep_m[0].astype(f32) + came_m[0].astype(f32)
    l_ref[...] = l
    sums_ref[:rank, :] = dot(l, l, 0, 0, HI)
    sums_ref[rank:, :] = dot(m2, l, 0, 0, HI)


def spread(row, col, m):
    return jnp.broadcast_to(row[:, col : col + 1], (8, m))


def eliminate(w_refs):
    m = w_refs[0].shape[0]

    def take(w, base):
        left = [jnp.broadcast_to(w[base + i : base + i + 1, :m], (8, m)) for i in range(8)]
        right = [jnp.broadcast_to(w[base + i : base + i + 1, m:], (8, m)) for i in range(8)]
        cell = [[spread(left[r], base + i, m) for i in range(r + 1)] for r in range(8)]
        return left, right, cell

    held = [take(w, 0) for w in w_refs]
    for base in range(0, m, 8):
        after = base + 8
        for at, w in enumerate(w_refs):
            left, right, cell = held[at]
            if after < m:
                next_left, next_right, next_cell = take(w, after)
            for i in range(8):
                inv = lax.rsqrt(cell[i][i])
                left[i] = left[i] * inv
                right[i] = right[i] * inv
                mult = [None] * 8
                for r in range(i + 1, 8):
                    mult[r] = cell[r][i] * inv
                for r in range(i + 1, 8):
                    for q in range(i + 1, r + 1):
                        cell[r][q] = cell[r][q] - mult[r] * mult[q]
                    left[r] = left[r] - mult[r] * left[i]
                    right[r] = right[r] - mult[r] * right[i]
                w[base + i : base + i + 1, :m] = left[i][:1, :]
                w[base + i : base + i + 1, m:] = right[i][:1, :]
                if after < m:
                    ahead = [spread(left[i], after + r, m) for r in range(8)]
                    for r in range(8):
                        for q in range(r + 1):
                            next_cell[r][q] = next_cell[r][q] - ahead[r] * ahead[q]
                        next_left[r] = next_left[r] - ahead[r] * left[i]
                        next_right[r] = next_right[r] - ahead[r] * right[i]
            if after + 8 < m:
                u = w[base:after, :]
                w[after + 8 :, :] -= dot(u[:, after + 8 : m], u, 0, 0, HI)
            if after < m:
                held[at] = (next_left, next_right, next_cell)


def load_gram(w, gram):
    m = gram.shape[0]
    row = lax.broadcasted_iota(i32, (m, m), 0)
    col = lax.broadcasted_iota(i32, (m, m), 1)
    w[:, :m] = gram
    w[:, m:] = jnp.where(row == col, 1.0, 0.0)


def upper(w):
    m = w.shape[0]
    row = lax.broadcasted_iota(i32, (m, m), 0)
    col = lax.broadcasted_iota(i32, (m, m), 1)
    return jnp.where(col >= row, w[:, :m], 0.0), jnp.where(col <= row, w[:, m:], 0.0)


def plans_lead_kernel(ss_ref, after, av_ref, w):
    load_gram(w, ss_ref[...])
    eliminate([w])
    av_ref[...] = upper(w)[1]


def lead_kernel(ratio, gram_ref, av_ref, lead_ref, w):
    m = av_ref.shape[0]
    load_gram(w, gram_ref[:m, :])
    av = av_ref[...]
    ck = gram_ref[m : 2 * m, :]
    l21v = dot(ck * ratio, av, 1, 1, HI)
    lead_ref[4] = av
    lead_ref[5] = l21v
    lead_ref[6] = dot(av, l21v, 0, 1, HI)
    lead_ref[7] = dot(l21v, l21v, 1, 1, HI)
    eliminate([w])
    a = upper(w)[1]
    l21u = dot(ck, a, 0, 1, HI)
    lead_ref[0] = a
    lead_ref[1] = l21u
    lead_ref[2] = dot(a, l21u, 0, 1, HI)
    lead_ref[3] = gram_ref[2 * m :, :] - dot(l21u, l21u, 1, 1, HI)


def cells_kernel(root, lead_ref, c_ref, k_ref, basis_ref, lt_ref, inv_ref, w):
    m = w.shape[0]
    load_gram(w, lead_ref[3])
    eliminate([w])
    lt, d = upper(w)
    lt_ref[...] = lt
    inv_ref[...] = d
    c = c_ref[...].astype(f32)
    basis_ref[:, :m] = dot(c, lead_ref[0], 1, 1, HI) * root
    basis_ref[:, m:] = dot(k_ref[...] - dot(c, lead_ref[2], 1, 0, HI), d, 1, 1, HI) * root


def plans_kernel(root, ck, cl, scale, sums_ref, lead_ref, ltu_ref, d_ref, s_ref, l_ref,
                 basis_ref, core_ref, w):
    m = w.shape[0]
    ll = sums_ref[:m, :]
    n22 = sums_ref[m:, :]
    load_gram(w, ll - lead_ref[7])
    eliminate([w])
    ltv, dv = upper(w)
    a, l21u, av, l21v, xv = (lead_ref[i] for i in (0, 1, 4, 5, 6))
    d = d_ref[...]
    own = s_ref[...].astype(f32)
    basis_ref[:, :m] = dot(own, av, 1, 1, HI) * root
    basis_ref[:, m:] = dot(l_ref[...] - dot(own, xv, 1, 0, HI), dv, 1, 1, HI) * root
    b = -dot(dot(d, l21u, 1, 0, HI), a, 1, 0, HI)
    e = dot(b, ll, 1, 0, HI) * (1.0 / cl) + dot(d, n22, 1, 0, HI) - dot(ltu_ref[...], xv, 1, 0, HI) * (1.0 / ck)
    core_ref[:m, :m] = dot(a, l21v, 1, 0, HI) * (scale / cl)
    core_ref[:m, m:] = dot(a, ltv, 1, 1, HI) * (scale / cl)
    core_ref[m:, :m] = dot(ltu_ref[...], av, 1, 1, HI) * (scale / ck)
    core_ref[m:, m:] = dot(e, dv, 1, 1, HI) * scale


def cost(units):
    return pl.CostEstimate(flops=0, bytes_accessed=units * 3_600_000, transcendentals=0)


def params(mib):
    return pltpu.CompilerParams(vmem_limit_bytes=mib << 20)


def local(cell_factor, sched_factor, core_matrix, rate_table, cell_well, sched_profile):
    cells_dev, rank = cell_factor.shape
    n_sched = sched_factor.shape[0]
    n = lax.axis_size("cell")
    n_cells = cells_dev * n
    profiles = rate_table.shape[1]
    me = lax.axis_index("cell")
    blk = n_sched // n
    bits = n.bit_length() - 1
    half = n // 2
    ck = PANEL_SCALE / n_sched
    cl = PANEL_SCALE / n_cells
    order_a = list(range(bits))
    order_b = [0, 2, 1] + order_a[3:] if bits > 2 else order_a

    def relative(j):
        return sum(((j >> (bits - 1 - i)) & 1) << bit for i, bit in enumerate(order_a))

    def slot_of(at):
        p = relative(at)
        return sum(((p >> bit) & 1) << (bits - 1 - i) for i, bit in enumerate(order_b) if i > 0)

    vmem = pl.BlockSpec(memory_space=pltpu.VMEM)
    hbm = pl.BlockSpec(memory_space=pltpu.HBM)
    anywhere = pl.BlockSpec(memory_space=pl.ANY)

    def shape(dtype, *dims):
        return jax.ShapeDtypeStruct(dims, dtype)

    part = shape(bf16, half, blk, rank)
    k, gram, send_l, send_m, hold_l, hold_m = pl.pallas_call(
        lambda *refs: state_kernel(ck, cl, relative, slot_of, *refs),
        out_shape=(shape(f32, cells_dev, rank), shape(f32, 3 * rank, rank), part, part, part, part),
        in_specs=[hbm] * 6,
        out_specs=(vmem,) * 2 + (hbm,) * 4,
        scratch_shapes=[
            pltpu.VMEM((cells_dev, rank), bf16),
            pltpu.VMEM((n, blk, rank), bf16),
            pltpu.VMEM((rank, rank), f32),
            pltpu.VMEM(rate_table.shape, bf16),
            pltpu.VMEM((1, cells_dev), i32),
            pltpu.VMEM((n, 1, blk), i32),
            pltpu.VMEM((n, blk, cells_dev), bf16),
            pltpu.VMEM((rank, cells_dev), bf16),
            pltpu.VMEM((profiles, rank), f32),
            pltpu.VMEM((rank, cells_dev), f32),
            pltpu.VMEM((cells_dev, 2 * rank), bf16),
            pltpu.VMEM((2 * profiles, 2 * rank), bf16),
            pltpu.VMEM((n, blk, rank), bf16),
            pltpu.VMEM((n, blk, rank), bf16),
            pltpu.SemaphoreType.DMA((6,)),
            pltpu.SemaphoreType.DMA((2, n)),
        ],
        compiler_params=params(60),
        name="state",
    )(
        cell_factor, sched_factor.reshape(n, blk, rank), core_matrix,
        rate_table, cell_well.reshape(1, cells_dev), sched_profile.reshape(n, 1, blk),
    )
    ss = dot(sched_factor, sched_factor, 0, 0)
    pair = pltpu.VMEM((rank, 2 * rank), f32)
    square = shape(f32, rank, rank)

    came_l, came_m = swap(send_l, 1, n), swap(send_m, 1, n)
    quarter = half // 2
    block = (1, blk, rank)
    near = pl.BlockSpec(block, lambda j: (j, 0, 0))
    far = pl.BlockSpec(block, lambda j: (quarter + j, 0, 0))
    part = shape(bf16, quarter, blk, rank)
    send_l, hold_l, send_m, hold_m = pl.pallas_call(
        first_fold_kernel, grid=(quarter,), out_shape=(part,) * 4,
        in_specs=[near, far] * 4, out_specs=(near,) * 4, compiler_params=params(20), name="first_fold",
    )(hold_l, hold_l, came_l, came_l, hold_m, hold_m, came_m, came_m)

    def fold(step, send_l, hold_l, send_m, hold_m, came_l, came_m, after):
        part = shape(bf16, half >> (step + 1), blk, rank)
        return pl.pallas_call(
            fold_kernel, out_shape=(part,) * 4, in_specs=[vmem] * 4 + [anywhere], out_specs=(vmem,) * 4,
            compiler_params=params(16), name="fold",
        )(hold_l, came_l, hold_m, came_m, after)

    came_l, came_m = swap(send_l, 1 << order_a[1], n), swap(send_m, 1 << order_b[1], n)
    gram = all_sum(gram, n)
    av = pl.pallas_call(
        plans_lead_kernel, out_shape=square, in_specs=[vmem, anywhere], out_specs=vmem,
        scratch_shapes=[pair], compiler_params=params(16), cost_estimate=cost(5), name="plans_lead",
    )(ss, hold_l)
    send_l, hold_l, send_m, hold_m = fold(1, send_l, hold_l, send_m, hold_m, came_l, came_m, av)
    for step in range(2, bits - 1):
        came_l = swap(send_l, 1 << order_a[step], n)
        came_m = swap(send_m, 1 << order_b[step], n)
        send_l, hold_l, send_m, hold_m = fold(step, send_l, hold_l, send_m, hold_m, came_l, came_m, av)
    came_l, came_m = swap(send_l, 1 << order_a[-1], n), swap(send_m, 1 << order_b[-1], n)
    lead = pl.pallas_call(
        lambda *refs: lead_kernel(cl / ck, *refs),
        out_shape=shape(f32, 8, rank, rank),
        in_specs=[vmem] * 2, out_specs=vmem, scratch_shapes=[pair],
        compiler_params=params(16), cost_estimate=cost(6), name="lead",
    )(gram, av)
    basis_cells, ltu, d = pl.pallas_call(
        lambda *refs: cells_kernel(float(n_cells) ** 0.5, *refs),
        out_shape=(shape(f32, cells_dev, 2 * rank), square, square),
        in_specs=[vmem] * 3, out_specs=(vmem,) * 3, scratch_shapes=[pair],
        compiler_params=params(16), cost_estimate=cost(8), name="cells",
    )(lead, cell_factor, k)
    lt, sums = pl.pallas_call(
        pair_kernel, out_shape=(shape(f32, blk, rank), shape(f32, 2 * rank, rank)),
        in_specs=[vmem] * 4 + [anywhere], out_specs=(vmem,) * 2,
        compiler_params=params(16), name="pair",
    )(hold_l, came_l, hold_m, came_m, av)
    sums = all_sum(sums, n)
    own = lax.dynamic_slice_in_dim(sched_factor, me * blk, blk, 0)
    scale = rank / (float(n_cells) * float(n_sched)) ** 0.5
    basis_sched, core_out = pl.pallas_call(
        lambda *refs: plans_kernel(float(n_sched) ** 0.5, ck, cl, scale, *refs),
        out_shape=(
            jax.ShapeDtypeStruct((blk, 2 * rank), f32),
            jax.ShapeDtypeStruct((2 * rank, 2 * rank), f32),
        ),
        in_specs=[vmem] * 6, out_specs=(vmem,) * 2, scratch_shapes=[pair],
        compiler_params=params(16), name="plans",
    )(sums, lead, ltu, d, own, lt)
    return (basis_cells, basis_sched, core_out)


def solution(mesh):
    return jax.shard_map(
        local,
        mesh=mesh,
        in_specs=(
            P(("group", "cell"), None),
            P("group", None),
            P("group", None),
            P(),
            P(("group", "cell")),
            P("group"),
        ),
        out_specs=(P(("group", "cell"), None), P(("group", "cell"), None), P("group", None)),
        check_vma=False,
    )
```

```python
import jax
import jax.numpy as jnp
from jax import lax
from jax.experimental import pallas as pl
from jax.experimental.pallas import tpu as pltpu
from jax.sharding import PartitionSpec as P

TIME_STEP = 0.25
PANEL_SCALE = 8.0
HI = lax.Precision.HIGHEST
f32, bf16, i32 = jnp.float32, jnp.bfloat16, jnp.int32


def dot(a, b, ca, cb, precision=None):
    return lax.dot_general(
        a, b, (((ca,), (cb,)), ((), ())), precision=precision, preferred_element_type=f32
    )


def split(x):
    hi = x.astype(bf16)
    return hi, (x - hi.astype(f32)).astype(bf16)


def dot3(a, b, ca, cb):
    a_hi, a_lo = split(a)
    b_hi, b_lo = split(b)
    return dot(a_hi, b_hi, ca, cb) + (dot(a_hi, b_lo, ca, cb) + dot(a_lo, b_hi, ca, cb))


def against(rows, inv, cross):
    hi, lo = split(jnp.concatenate([inv.T, cross], axis=1))
    return dot(rows, hi, 1, 0) + dot(rows, lo, 1, 0)


def swap(x, mask, n):
    return lax.ppermute(x, "cell", [(i, i ^ mask) for i in range(n)])


def diagonal(m):
    return lax.broadcasted_iota(i32, (m, m), 0) - lax.broadcasted_iota(i32, (m, m), 1)


def cut(rows_ref, send_ref, keep_ref):
    half = send_ref.shape[0]
    odd = lax.rem(lax.axis_index("cell"), 2)
    send_ref[...] = rows_ref[pl.ds(pl.multiple_of((1 - odd) * half, 8), half), :]
    keep_ref[...] = rows_ref[pl.ds(pl.multiple_of(odd * half, 8), half), :]


def joined(rows_ref, mine_ref, other_ref):
    half = mine_ref.shape[0]
    odd = lax.rem(lax.axis_index("cell"), 2)
    rows_ref[pl.ds(pl.multiple_of(odd * half, 8), half), :] = mine_ref[...]
    rows_ref[pl.ds(pl.multiple_of((1 - odd) * half, 8), half), :] = other_ref[...]


def state_kernel(ck, cl, relative, slot_of, c_hbm, s_hbm, core_hbm, table_hbm, well_hbm, prof_hbm,
                 k_ref, gsend_ref, gkeep_ref, send_l, send_m, hold_l, hold_m,
                 c_ref, s_ref, core_ref, table_ref, well_ref, prof_ref,
                 g_ref, ft_ref, ps_ref, kt_ref, both_ref, inj_ref, l_ref, m_ref, gram_ref, sems, out_sems):
    n, blk, rank = s_ref.shape
    cells = c_ref.shape[0]
    half = n // 2
    wells, profiles = table_ref.shape
    copies = [
        pltpu.make_async_copy(src, dst, sems.at[i])
        for i, (src, dst) in enumerate(
            [(c_hbm, c_ref), (core_hbm, core_ref), (s_hbm, s_ref), (prof_hbm, prof_ref),
             (table_hbm, table_ref), (well_hbm, well_ref)]
        )
    ]
    for copy in copies:
        copy.start()
    kt_ref[...] = jnp.zeros_like(kt_ref)
    ps_ref[...] = jnp.zeros_like(ps_ref)
    copies[0].wait()
    copies[1].wait()
    c = c_ref[...]
    core = core_ref[...]
    c1 = core.astype(bf16)
    c2, c3 = split(core - c1.astype(f32))
    ft_ref[...] = (dot(c, c1, 1, 0) + dot(c, c2, 1, 0) + dot(c, c3, 1, 0)).T.astype(bf16)
    for copy in copies[2:]:
        copy.wait()

    def first(b, carry):
        s = s_ref[b]
        r = dot(s, ft_ref[...], 1, 0)
        g = (r * ((1.0 + TIME_STEP) - TIME_STEP * (r * r))).astype(bf16)
        g_ref[b] = g
        kt_ref[...] += dot(s, g, 0, 0)
        ps_ref[...] += dot(onehot(prof_ref[b], profiles, blk), s, 1, 0)
        return carry

    lax.fori_loop(0, n, first, 0, unroll=2)

    table = table_ref[...]
    wt = onehot(well_ref[...], wells, cells)
    ps_hi, ps_lo = split(ps_ref[...])
    tp_hi, tp_lo = split(dot(table, ps_hi, 1, 0) + dot(table, ps_lo, 1, 0))
    kt = (kt_ref[...] + TIME_STEP * (dot(tp_hi, wt, 0, 0) + dot(tp_lo, wt, 0, 0))) * ck
    k = kt.T
    k_ref[...] = k
    ct = c.astype(f32).T.astype(bf16)
    kt_hi, kt_lo = split(kt)
    k_hi, k_lo = split(k)
    both_ref[:, :rank] = c
    both_ref[:, rank:] = k_hi
    w_hi, w_lo = split(dot(wt, both_ref[...], 1, 0))
    a_hi, a_lo = split(TIME_STEP * (dot(table, w_hi, 0, 0) + dot(table, w_lo, 0, 0)))
    inj_ref[:profiles, :] = a_hi
    inj_ref[profiles:, :] = a_lo
    cc = dot(ct, c, 1, 0)
    kk = dot(kt_hi, k_hi, 1, 0) + (dot(kt_hi, k_lo, 1, 0) + dot(kt_lo, k_hi, 1, 0))
    below = diagonal(rank)
    gram_ref[:rank, :] = dot(ct, k_hi, 1, 0) + dot(ct, k_lo, 1, 0)
    gram_ref[rank : 2 * rank, :] = jnp.where(below > 0, cc, kk)
    gram_ref[2 * rank :, :] = jnp.broadcast_to(
        jnp.sum(jnp.where(below == 0, cc, 0.0), axis=0, keepdims=True), (16, rank)
    )
    cut(gram_ref, gsend_ref, gkeep_ref)
    me = lax.axis_index("cell")

    def outgoing(j, at, dst_l, dst_m):
        return (
            pltpu.make_async_copy(l_ref.at[j], dst_l.at[at], out_sems.at[0, j]),
            pltpu.make_async_copy(m_ref.at[j], dst_m.at[slot_of(at)], out_sems.at[1, j]),
        )

    def second(first_slot, dst_l, dst_m):
        def body(at, carry):
            j = first_slot + at
            b = me ^ relative(j)
            hot = onehot(prof_ref[b], profiles, blk)
            out = dot(g_ref[b], both_ref[...], 1, 0) + dot(
                jnp.concatenate([hot, hot], axis=0), inj_ref[...], 0, 0
            )
            l_ref[j] = (out[:, :rank] * cl).astype(bf16)
            m_ref[j] = out[:, rank:].astype(bf16)
            for copy in outgoing(j, at, dst_l, dst_m):
                copy.start()
            return carry

        lax.fori_loop(0, half, body, 0, unroll=2)

    def finish(first_slot, dst_l, dst_m):
        def body(at, carry):
            for copy in outgoing(first_slot + at, at, dst_l, dst_m):
                copy.wait()
            return carry

        lax.fori_loop(0, half, body, 0)

    second(half, send_l, send_m)
    second(0, hold_l, hold_m)
    finish(half, send_l, send_m)
    finish(0, hold_l, hold_m)


def onehot(ids, size, count):
    return jnp.where(lax.broadcasted_iota(i32, (size, count), 0) == ids, 1.0, 0.0).astype(bf16)


def fold_kernel(keep_l, came_l, keep_m, came_m, after, send_l, hold_l, send_m, hold_m):
    half = hold_l.shape[0]
    for keep, came, send, hold in ((keep_l, came_l, send_l, hold_l), (keep_m, came_m, send_m, hold_m)):
        for j in range(half):
            hold[j] = (keep[j].astype(f32) + came[j].astype(f32)).astype(bf16)
            send[j] = (keep[half + j].astype(f32) + came[half + j].astype(f32)).astype(bf16)


def first_fold_kernel(keep_l0, keep_l1, came_l0, came_l1, keep_m0, keep_m1, came_m0, came_m1,
                      send_l, hold_l, send_m, hold_m):
    for keep, came, out in (
        (keep_l0, came_l0, hold_l), (keep_l1, came_l1, send_l),
        (keep_m0, came_m0, hold_m), (keep_m1, came_m1, send_m),
    ):
        out[...] = (keep[...].astype(f32) + came[...].astype(f32)).astype(bf16)


def pair_kernel(keep_l, came_l, keep_m, came_m, after, l_ref, send_ref, keep_ref, sums_ref):
    rank = l_ref.shape[1]
    l = keep_l[0].astype(f32) + came_l[0].astype(f32)
    m2 = keep_m[0].astype(f32) + came_m[0].astype(f32)
    l_ref[...] = l
    sums_ref[:rank, :] = dot(l, l, 0, 0, HI)
    sums_ref[rank:, :] = dot(m2, l, 0, 0, HI)
    cut(sums_ref, send_ref, keep_ref)


def add_kernel(a_ref, b_ref, after, out_ref):
    out_ref[...] = a_ref[...] + b_ref[...]


def spread(row, col, m):
    return jnp.broadcast_to(row[:, col : col + 1], (8, m))


def eliminate(w_refs):
    m = w_refs[0].shape[0]

    def take(w, base):
        left = [jnp.broadcast_to(w[base + i : base + i + 1, :m], (8, m)) for i in range(8)]
        right = [jnp.broadcast_to(w[base + i : base + i + 1, m:], (8, m)) for i in range(8)]
        cell = [[spread(left[r], base + i, m) for i in range(r + 1)] for r in range(8)]
        return left, right, cell

    held = [take(w, 0) for w in w_refs]
    for base in range(0, m, 8):
        after = base + 8
        for at, w in enumerate(w_refs):
            left, right, cell = held[at]
            if after < m:
                next_left, next_right, next_cell = take(w, after)
            for i in range(8):
                inv = lax.rsqrt(cell[i][i])
                left[i] = left[i] * inv
                right[i] = right[i] * inv
                mult = [None] * 8
                for r in range(i + 1, 8):
                    mult[r] = cell[r][i] * inv
                for r in range(i + 1, 8):
                    for q in range(i + 1, r + 1):
                        cell[r][q] = cell[r][q] - mult[r] * mult[q]
                    left[r] = left[r] - mult[r] * left[i]
                    right[r] = right[r] - mult[r] * right[i]
                w[base + i : base + i + 1, :m] = left[i][:1, :]
                w[base + i : base + i + 1, m:] = right[i][:1, :]
                if after < m:
                    ahead = [spread(left[i], after + r, m) for r in range(8)]
                    for r in range(8):
                        for q in range(r + 1):
                            next_cell[r][q] = next_cell[r][q] - ahead[r] * ahead[q]
                        next_left[r] = next_left[r] - ahead[r] * left[i]
                        next_right[r] = next_right[r] - ahead[r] * right[i]
            if after + 8 < m:
                u = w[base:after, :]
                w[after + 8 :, :] -= dot(u[:, after + 8 : m], u, 0, 0, HI)
            if after < m:
                held[at] = (next_left, next_right, next_cell)


def load_gram(w, gram):
    m = gram.shape[0]
    row = lax.broadcasted_iota(i32, (m, m), 0)
    col = lax.broadcasted_iota(i32, (m, m), 1)
    w[:, :m] = gram
    w[:, m:] = jnp.where(row == col, 1.0, 0.0)


def upper(w):
    m = w.shape[0]
    row = lax.broadcasted_iota(i32, (m, m), 0)
    col = lax.broadcasted_iota(i32, (m, m), 1)
    return jnp.where(col >= row, w[:, :m], 0.0), jnp.where(col <= row, w[:, m:], 0.0)


def plans_lead_kernel(ss_ref, after, av_ref, w):
    load_gram(w, ss_ref[...])
    eliminate([w])
    av_ref[...] = upper(w)[1]


def lead_kernel(ratio, mine_ref, other_ref, av_ref, lead_ref, w, gram_ref):
    m = av_ref.shape[0]
    joined(gram_ref, mine_ref, other_ref)
    below = diagonal(m)
    mixed = gram_ref[m : 2 * m, :]
    low = jnp.where(below > 0, mixed, 0.0)
    high = jnp.where(below <= 0, mixed, 0.0)
    strict = jnp.where(below < 0, mixed, 0.0)
    load_gram(w, low + low.T + jnp.where(below == 0, gram_ref[2 * m : 2 * m + 1, :], 0.0))
    av = av_ref[...]
    ck = gram_ref[:m, :]
    l21v = dot(ck * ratio, av, 1, 1, HI)
    lead_ref[4] = av
    lead_ref[5] = l21v
    lead_ref[6] = dot(av, l21v, 0, 1, HI)
    lead_ref[7] = dot(l21v, l21v, 1, 1, HI)
    eliminate([w])
    a = upper(w)[1]
    l21u = dot(ck, a, 0, 1, HI)
    lead_ref[0] = a
    lead_ref[1] = l21u
    lead_ref[2] = dot(a, l21u, 0, 1, HI)
    lead_ref[3] = high + strict.T - dot(l21u, l21u, 1, 1, HI)


def cells_kernel(root, lead_ref, c_ref, k_ref, basis_ref, lt_ref, inv_ref, w):
    m = w.shape[0]
    load_gram(w, lead_ref[3])
    both = against(c_ref[...], lead_ref[0], lead_ref[2])
    basis_ref[:, :m] = both[:, :m] * root
    basis_ref[:, m:] = k_ref[...] - both[:, m:]
    eliminate([w])
    lt, d = upper(w)
    lt_ref[...] = lt
    inv_ref[...] = d
    basis_ref[:, m:] = dot3(basis_ref[:, m:], d * root, 1, 1)


def plans_kernel(root, ck, cl, scale, mine_ref, other_ref, lead_ref, ltu_ref, d_ref, s_ref, l_ref,
                 basis_ref, core_ref, w, sums_ref):
    m = w.shape[0]
    joined(sums_ref, mine_ref, other_ref)
    ll = sums_ref[:m, :]
    n22 = sums_ref[m:, :]
    load_gram(w, ll - lead_ref[7])
    a, l21u, av, l21v, xv = (lead_ref[i] for i in (0, 1, 4, 5, 6))
    d = d_ref[...]
    both = against(s_ref[...], av, xv)
    basis_ref[:, :m] = both[:, :m] * root
    basis_ref[:, m:] = l_ref[...] - both[:, m:]
    b = -dot(dot(d, l21u, 1, 0, HI), a, 1, 0, HI)
    core_ref[m:, m:] = (
        dot(b, ll, 1, 0, HI) * (1.0 / cl) + dot(d, n22, 1, 0, HI)
        - dot(ltu_ref[...], xv, 1, 0, HI) * (1.0 / ck)
    )
    core_ref[:m, :m] = dot(a, l21v, 1, 0, HI) * (scale / cl)
    core_ref[m:, :m] = dot(ltu_ref[...], av, 1, 1, HI) * (scale / ck)
    eliminate([w])
    ltv, dv = upper(w)
    basis_ref[:, m:] = dot3(basis_ref[:, m:], dv * root, 1, 1)
    core_ref[:m, m:] = dot(a, ltv, 1, 1, HI) * (scale / cl)
    core_ref[m:, m:] = dot(core_ref[m:, m:], dv, 1, 1, HI) * scale


def cost(units):
    return pl.CostEstimate(flops=0, bytes_accessed=units * 3_600_000, transcendentals=0)


def params(mib):
    return pltpu.CompilerParams(vmem_limit_bytes=mib << 20)


def local(cell_factor, sched_factor, core_matrix, rate_table, cell_well, sched_profile):
    cells_dev, rank = cell_factor.shape
    n_sched = sched_factor.shape[0]
    n = lax.axis_size("cell")
    n_cells = cells_dev * n
    profiles = rate_table.shape[1]
    me = lax.axis_index("cell")
    blk = n_sched // n
    bits = n.bit_length() - 1
    half = n // 2
    ck = PANEL_SCALE / n_sched
    cl = PANEL_SCALE / n_cells
    order_a = list(range(bits))
    order_b = [0, 2, 1] + order_a[3:] if bits > 2 else order_a

    def relative(j):
        return sum(((j >> (bits - 1 - i)) & 1) << bit for i, bit in enumerate(order_a))

    def slot_of(at):
        p = relative(at)
        return sum(((p >> bit) & 1) << (bits - 1 - i) for i, bit in enumerate(order_b) if i > 0)

    vmem = pl.BlockSpec(memory_space=pltpu.VMEM)
    hbm = pl.BlockSpec(memory_space=pltpu.HBM)
    anywhere = pl.BlockSpec(memory_space=pl.ANY)

    def shape(dtype, *dims):
        return jax.ShapeDtypeStruct(dims, dtype)

    part = shape(bf16, half, blk, rank)
    gram_half = shape(f32, rank + 8, rank)
    k, gram_send, gram, send_l, send_m, hold_l, hold_m = pl.pallas_call(
        lambda *refs: state_kernel(ck, cl, relative, slot_of, *refs),
        out_shape=(shape(f32, cells_dev, rank), gram_half, gram_half, part, part, part, part),
        in_specs=[hbm] * 6,
        out_specs=(vmem,) * 3 + (hbm,) * 4,
        scratch_shapes=[
            pltpu.VMEM((cells_dev, rank), bf16),
            pltpu.VMEM((n, blk, rank), bf16),
            pltpu.VMEM((rank, rank), f32),
            pltpu.VMEM(rate_table.shape, bf16),
            pltpu.VMEM((1, cells_dev), i32),
            pltpu.VMEM((n, 1, blk), i32),
            pltpu.VMEM((n, blk, cells_dev), bf16),
            pltpu.VMEM((rank, cells_dev), bf16),
            pltpu.VMEM((profiles, rank), f32),
            pltpu.VMEM((rank, cells_dev), f32),
            pltpu.VMEM((cells_dev, 2 * rank), bf16),
            pltpu.VMEM((2 * profiles, 2 * rank), bf16),
            pltpu.VMEM((n, blk, rank), bf16),
            pltpu.VMEM((n, blk, rank), bf16),
            pltpu.VMEM((2 * rank + 16, rank), f32),
            pltpu.SemaphoreType.DMA((6,)),
            pltpu.SemaphoreType.DMA((2, n)),
        ],
        compiler_params=params(60),
        name="state",
    )(
        cell_factor, sched_factor.reshape(n, blk, rank), core_matrix,
        rate_table, cell_well.reshape(1, cells_dev), sched_profile.reshape(n, 1, blk),
    )
    ss = dot(sched_factor, sched_factor, 0, 0)
    pair = pltpu.VMEM((rank, 2 * rank), f32)
    square = shape(f32, rank, rank)

    came_l, came_m = swap(send_l, 1, n), swap(send_m, 1, n)
    gram = gram + swap(gram_send, 1, n)
    quarter = half // 2
    block = (1, blk, rank)
    near = pl.BlockSpec(block, lambda j: (j, 0, 0))
    far = pl.BlockSpec(block, lambda j: (quarter + j, 0, 0))
    part = shape(bf16, quarter, blk, rank)
    send_l, hold_l, send_m, hold_m = pl.pallas_call(
        first_fold_kernel, grid=(quarter,), out_shape=(part,) * 4,
        in_specs=[near, far] * 4, out_specs=(near,) * 4, compiler_params=params(20), name="first_fold",
    )(hold_l, hold_l, came_l, came_l, hold_m, hold_m, came_m, came_m)

    def fold(step, send_l, hold_l, send_m, hold_m, came_l, came_m, after):
        part = shape(bf16, half >> (step + 1), blk, rank)
        return pl.pallas_call(
            fold_kernel, out_shape=(part,) * 4, in_specs=[vmem] * 4 + [anywhere], out_specs=(vmem,) * 4,
            compiler_params=params(16), name="fold",
        )(hold_l, came_l, hold_m, came_m, after)

    came_l, came_m = swap(send_l, 1 << order_a[1], n), swap(send_m, 1 << order_b[1], n)
    for bit in range(1, bits):
        gram = gram + swap(gram, 1 << bit, n)
    gram_other = swap(gram, 1, n)
    av = pl.pallas_call(
        plans_lead_kernel, out_shape=square, in_specs=[vmem, anywhere], out_specs=vmem,
        scratch_shapes=[pair], compiler_params=params(16), cost_estimate=cost(5), name="plans_lead",
    )(ss, hold_l)
    send_l, hold_l, send_m, hold_m = fold(1, send_l, hold_l, send_m, hold_m, came_l, came_m, av)
    for step in range(2, bits - 1):
        came_l = swap(send_l, 1 << order_a[step], n)
        came_m = swap(send_m, 1 << order_b[step], n)
        send_l, hold_l, send_m, hold_m = fold(step, send_l, hold_l, send_m, hold_m, came_l, came_m, av)
    came_l, came_m = swap(send_l, 1 << order_a[-1], n), swap(send_m, 1 << order_b[-1], n)
    lead = pl.pallas_call(
        lambda *refs: lead_kernel(cl / ck, *refs),
        out_shape=shape(f32, 8, rank, rank),
        in_specs=[vmem] * 3, out_specs=vmem,
        scratch_shapes=[pair, pltpu.VMEM((2 * rank + 16, rank), f32)],
        compiler_params=params(16), cost_estimate=cost(6), name="lead",
    )(gram, gram_other, av)
    basis_cells, ltu, d = pl.pallas_call(
        lambda *refs: cells_kernel(float(n_cells) ** 0.5, *refs),
        out_shape=(shape(f32, cells_dev, 2 * rank), square, square),
        in_specs=[vmem] * 3, out_specs=(vmem,) * 3, scratch_shapes=[pair],
        compiler_params=params(16), cost_estimate=cost(8), name="cells",
    )(lead, cell_factor, k)
    lt, sums_send, sums = pl.pallas_call(
        pair_kernel, out_shape=(shape(f32, blk, rank), square, square),
        in_specs=[vmem] * 4 + [anywhere], out_specs=(vmem,) * 3,
        scratch_shapes=[pltpu.VMEM((2 * rank, rank), f32)],
        compiler_params=params(16), name="pair",
    )(hold_l, came_l, hold_m, came_m, av)
    sums = sums + swap(sums_send, 1, n)
    dues = [lead] * (bits - 2) + [d]
    for bit, due in zip(range(1, bits), dues):
        sums = pl.pallas_call(
            add_kernel, out_shape=square, in_specs=[vmem] * 2 + [anywhere], out_specs=vmem,
            compiler_params=params(16), name="add",
        )(sums, swap(sums, 1 << bit, n), due)
    sums_other = swap(sums, 1, n)
    own = lax.dynamic_slice_in_dim(sched_factor, me * blk, blk, 0)
    scale = rank / (float(n_cells) * float(n_sched)) ** 0.5
    basis_sched, core_out = pl.pallas_call(
        lambda *refs: plans_kernel(float(n_sched) ** 0.5, ck, cl, scale, *refs),
        out_shape=(
            jax.ShapeDtypeStruct((blk, 2 * rank), f32),
            jax.ShapeDtypeStruct((2 * rank, 2 * rank), f32),
        ),
        in_specs=[vmem] * 7, out_specs=(vmem,) * 2,
        scratch_shapes=[pair, pltpu.VMEM((2 * rank, rank), f32)],
        compiler_params=params(16), name="plans",
    )(sums, sums_other, lead, ltu, d, own, lt)
    return (basis_cells, basis_sched, core_out)


def solution(mesh):
    return jax.shard_map(
        local,
        mesh=mesh,
        in_specs=(
            P(("group", "cell"), None),
            P("group", None),
            P("group", None),
            P(),
            P(("group", "cell")),
            P("group"),
        ),
        out_specs=(P(("group", "cell"), None), P(("group", "cell"), None), P("group", None)),
        check_vma=False,
    )
```

```python
import jax
import jax.numpy as jnp
from jax import lax
from jax.experimental import pallas as pl
from jax.experimental.pallas import tpu as pltpu
from jax.sharding import PartitionSpec as P

TIME_STEP = 0.25
PANEL_SCALE = 8.0
HI = lax.Precision.HIGHEST
f32, bf16, i32 = jnp.float32, jnp.bfloat16, jnp.int32


def dot(a, b, ca, cb, precision=None):
    return lax.dot_general(
        a, b, (((ca,), (cb,)), ((), ())), precision=precision, preferred_element_type=f32
    )


def split(x):
    hi = x.astype(bf16)
    return hi, (x - hi.astype(f32)).astype(bf16)


def dot3(a, b, ca, cb):
    a_hi, a_lo = split(a)
    b_hi, b_lo = split(b)
    return dot(a_hi, b_hi, ca, cb) + (dot(a_hi, b_lo, ca, cb) + dot(a_lo, b_hi, ca, cb))


def against(rows, inv, cross):
    hi, lo = split(jnp.concatenate([inv.T, cross], axis=1))
    return dot(rows, hi, 1, 0) + dot(rows, lo, 1, 0)


def swap(x, mask, n):
    return lax.ppermute(x, "cell", [(i, i ^ mask) for i in range(n)])


def diagonal(m):
    return lax.broadcasted_iota(i32, (m, m), 0) - lax.broadcasted_iota(i32, (m, m), 1)


def cut(rows_ref, send_ref, keep_ref):
    half = send_ref.shape[0]
    odd = lax.rem(lax.axis_index("cell"), 2)
    send_ref[...] = rows_ref[pl.ds(pl.multiple_of((1 - odd) * half, 8), half), :]
    keep_ref[...] = rows_ref[pl.ds(pl.multiple_of(odd * half, 8), half), :]


def joined(rows_ref, mine_ref, other_ref):
    half = mine_ref.shape[0]
    odd = lax.rem(lax.axis_index("cell"), 2)
    rows_ref[pl.ds(pl.multiple_of(odd * half, 8), half), :] = mine_ref[...]
    rows_ref[pl.ds(pl.multiple_of((1 - odd) * half, 8), half), :] = other_ref[...]


def state_kernel(ck, cl, relative, slot_of, c_hbm, s_hbm, core_hbm, table_hbm, well_hbm, prof_hbm,
                 k_ref, gsend_ref, gkeep_ref, send_l, send_m, hold_l, hold_m,
                 c_ref, s_ref, core_ref, table_ref, well_ref, prof_ref,
                 g_ref, ft_ref, ps_ref, kt_ref, both_ref, inj_ref, l_ref, m_ref, gram_ref, sems, out_sems):
    n, blk, rank = s_ref.shape
    cells = c_ref.shape[0]
    half = n // 2
    wells, profiles = table_ref.shape
    copies = [
        pltpu.make_async_copy(src, dst, sems.at[i])
        for i, (src, dst) in enumerate(
            [(c_hbm, c_ref), (core_hbm, core_ref), (s_hbm, s_ref), (prof_hbm, prof_ref),
             (table_hbm, table_ref), (well_hbm, well_ref)]
        )
    ]
    for copy in copies:
        copy.start()
    kt_ref[...] = jnp.zeros_like(kt_ref)
    ps_ref[...] = jnp.zeros_like(ps_ref)
    copies[0].wait()
    copies[1].wait()
    c = c_ref[...]
    core = core_ref[...]
    c1 = core.astype(bf16)
    c2, c3 = split(core - c1.astype(f32))
    ft_ref[...] = (dot(c, c1, 1, 0) + dot(c, c2, 1, 0) + dot(c, c3, 1, 0)).T.astype(bf16)
    for copy in copies[2:]:
        copy.wait()

    def first(b, carry):
        s = s_ref[b]
        r = dot(s, ft_ref[...], 1, 0)
        g = (r * ((1.0 + TIME_STEP) - TIME_STEP * (r * r))).astype(bf16)
        g_ref[b] = g
        kt_ref[...] += dot(s, g, 0, 0)
        ps_ref[...] += dot(onehot(prof_ref[b], profiles, blk), s, 1, 0)
        return carry

    lax.fori_loop(0, n, first, 0, unroll=4)

    table = table_ref[...]
    wt = onehot(well_ref[...], wells, cells)
    ps_hi, ps_lo = split(ps_ref[...])
    tp_hi, tp_lo = split(dot(table, ps_hi, 1, 0) + dot(table, ps_lo, 1, 0))
    kt = (kt_ref[...] + TIME_STEP * (dot(tp_hi, wt, 0, 0) + dot(tp_lo, wt, 0, 0))) * ck
    k = kt.T
    k_ref[...] = k
    ct = c.astype(f32).T.astype(bf16)
    kt_hi, kt_lo = split(kt)
    k_hi, k_lo = split(k)
    both_ref[:, :rank] = c
    both_ref[:, rank:] = k_hi
    w_hi, w_lo = split(dot(wt, both_ref[...], 1, 0))
    a_hi, a_lo = split(TIME_STEP * (dot(table, w_hi, 0, 0) + dot(table, w_lo, 0, 0)))
    inj_ref[:profiles, :] = a_hi
    inj_ref[profiles:, :] = a_lo
    cc = dot(ct, c, 1, 0)
    kk = dot(kt_hi, k_hi, 1, 0) + (dot(kt_hi, k_lo, 1, 0) + dot(kt_lo, k_hi, 1, 0))
    below = diagonal(rank)
    gram_ref[:rank, :] = dot(ct, k_hi, 1, 0) + dot(ct, k_lo, 1, 0)
    gram_ref[rank : 2 * rank, :] = jnp.where(below > 0, cc, kk)
    gram_ref[2 * rank :, :] = jnp.broadcast_to(
        jnp.sum(jnp.where(below == 0, cc, 0.0), axis=0, keepdims=True), (16, rank)
    )
    cut(gram_ref, gsend_ref, gkeep_ref)
    me = lax.axis_index("cell")

    def outgoing(j, at, dst_l, dst_m):
        return (
            pltpu.make_async_copy(l_ref.at[j], dst_l.at[at], out_sems.at[0, j]),
            pltpu.make_async_copy(m_ref.at[j], dst_m.at[slot_of(at)], out_sems.at[1, j]),
        )

    def second(first_slot, dst_l, dst_m):
        def body(at, carry):
            j = first_slot + at
            b = me ^ relative(j)
            hot = onehot(prof_ref[b], profiles, blk)
            out = dot(g_ref[b], both_ref[...], 1, 0) + dot(
                jnp.concatenate([hot, hot], axis=0), inj_ref[...], 0, 0
            )
            l_ref[j] = (out[:, :rank] * cl).astype(bf16)
            m_ref[j] = out[:, rank:].astype(bf16)
            for copy in outgoing(j, at, dst_l, dst_m):
                copy.start()
            return carry

        lax.fori_loop(0, half, body, 0, unroll=4)

    def finish(first_slot, dst_l, dst_m):
        def body(at, carry):
            for copy in outgoing(first_slot + at, at, dst_l, dst_m):
                copy.wait()
            return carry

        lax.fori_loop(0, half, body, 0)

    second(half, send_l, send_m)
    second(0, hold_l, hold_m)
    finish(half, send_l, send_m)
    finish(0, hold_l, hold_m)


def onehot(ids, size, count):
    return jnp.where(lax.broadcasted_iota(i32, (size, count), 0) == ids, 1.0, 0.0).astype(bf16)


def fold_kernel(keep_l, came_l, keep_m, came_m, after, send_l, hold_l, send_m, hold_m):
    half = hold_l.shape[0]
    for keep, came, send, hold in ((keep_l, came_l, send_l, hold_l), (keep_m, came_m, send_m, hold_m)):
        for j in range(half):
            hold[j] = (keep[j].astype(f32) + came[j].astype(f32)).astype(bf16)
            send[j] = (keep[half + j].astype(f32) + came[half + j].astype(f32)).astype(bf16)


def first_fold_kernel(keep_l0, keep_l1, came_l0, came_l1, keep_m0, keep_m1, came_m0, came_m1,
                      send_l, hold_l, send_m, hold_m):
    for keep, came, out in (
        (keep_l0, came_l0, hold_l), (keep_l1, came_l1, send_l),
        (keep_m0, came_m0, hold_m), (keep_m1, came_m1, send_m),
    ):
        out[...] = (keep[...].astype(f32) + came[...].astype(f32)).astype(bf16)


def pair_kernel(keep_l, came_l, keep_m, came_m, after, l_ref, send_ref, keep_ref, sums_ref):
    rank = l_ref.shape[1]
    l = keep_l[0].astype(f32) + came_l[0].astype(f32)
    m2 = keep_m[0].astype(f32) + came_m[0].astype(f32)
    l_ref[...] = l
    sums_ref[:rank, :] = dot(l, l, 0, 0, HI)
    sums_ref[rank:, :] = dot(m2, l, 0, 0, HI)
    cut(sums_ref, send_ref, keep_ref)


def add_kernel(a_ref, b_ref, after, out_ref):
    out_ref[...] = a_ref[...] + b_ref[...]


def spread(row, col, m):
    return jnp.broadcast_to(row[:, col : col + 1], (8, m))


def eliminate(w_refs):
    m = w_refs[0].shape[0]

    def take(w, base):
        left = [jnp.broadcast_to(w[base + i : base + i + 1, :m], (8, m)) for i in range(8)]
        right = [jnp.broadcast_to(w[base + i : base + i + 1, m:], (8, m)) for i in range(8)]
        cell = [[spread(left[r], base + i, m) for i in range(r + 1)] for r in range(8)]
        return left, right, cell

    held = [take(w, 0) for w in w_refs]
    for base in range(0, m, 8):
        after = base + 8
        for at, w in enumerate(w_refs):
            left, right, cell = held[at]
            if after < m:
                next_left, next_right, next_cell = take(w, after)
            for i in range(8):
                inv = lax.rsqrt(cell[i][i])
                left[i] = left[i] * inv
                right[i] = right[i] * inv
                mult = [None] * 8
                for r in range(i + 1, 8):
                    mult[r] = cell[r][i] * inv
                for r in range(i + 1, 8):
                    for q in range(i + 1, r + 1):
                        cell[r][q] = cell[r][q] - mult[r] * mult[q]
                    left[r] = left[r] - mult[r] * left[i]
                    right[r] = right[r] - mult[r] * right[i]
                w[base + i : base + i + 1, :m] = left[i][:1, :]
                w[base + i : base + i + 1, m:] = right[i][:1, :]
                if after < m:
                    ahead = [spread(left[i], after + r, m) for r in range(8)]
                    for r in range(8):
                        for q in range(r + 1):
                            next_cell[r][q] = next_cell[r][q] - ahead[r] * ahead[q]
                        next_left[r] = next_left[r] - ahead[r] * left[i]
                        next_right[r] = next_right[r] - ahead[r] * right[i]
            if after + 8 < m:
                u = w[base:after, :]
                w[after + 8 :, :] -= dot(u[:, after + 8 : m], u, 0, 0, HI)
            if after < m:
                held[at] = (next_left, next_right, next_cell)


def load_gram(w, gram):
    m = gram.shape[0]
    row = lax.broadcasted_iota(i32, (m, m), 0)
    col = lax.broadcasted_iota(i32, (m, m), 1)
    w[:, :m] = gram
    w[:, m:] = jnp.where(row == col, 1.0, 0.0)


def upper(w):
    m = w.shape[0]
    row = lax.broadcasted_iota(i32, (m, m), 0)
    col = lax.broadcasted_iota(i32, (m, m), 1)
    return jnp.where(col >= row, w[:, :m], 0.0), jnp.where(col <= row, w[:, m:], 0.0)


def plans_lead_kernel(ss_ref, after, av_ref, w):
    load_gram(w, ss_ref[...])
    eliminate([w])
    av_ref[...] = upper(w)[1]


def lead_kernel(ratio, mine_ref, other_ref, av_ref, lead_ref, w, gram_ref):
    m = av_ref.shape[0]
    joined(gram_ref, mine_ref, other_ref)
    below = diagonal(m)
    mixed = gram_ref[m : 2 * m, :]
    low = jnp.where(below > 0, mixed, 0.0)
    high = jnp.where(below <= 0, mixed, 0.0)
    strict = jnp.where(below < 0, mixed, 0.0)
    load_gram(w, low + low.T + jnp.where(below == 0, gram_ref[2 * m : 2 * m + 1, :], 0.0))
    av = av_ref[...]
    ck = gram_ref[:m, :]
    l21v = dot(ck * ratio, av, 1, 1, HI)
    lead_ref[4] = av
    lead_ref[5] = l21v
    lead_ref[6] = dot(av, l21v, 0, 1, HI)
    lead_ref[7] = dot(l21v, l21v, 1, 1, HI)
    eliminate([w])
    a = upper(w)[1]
    l21u = dot(ck, a, 0, 1, HI)
    lead_ref[0] = a
    lead_ref[1] = l21u
    lead_ref[2] = dot(a, l21u, 0, 1, HI)
    lead_ref[3] = high + strict.T - dot(l21u, l21u, 1, 1, HI)


def cells_kernel(root, lead_ref, c_ref, k_ref, basis_ref, lt_ref, inv_ref, w):
    m = w.shape[0]
    load_gram(w, lead_ref[3])
    both = against(c_ref[...], lead_ref[0], lead_ref[2])
    basis_ref[:, :m] = both[:, :m] * root
    basis_ref[:, m:] = k_ref[...] - both[:, m:]
    eliminate([w])
    lt, d = upper(w)
    lt_ref[...] = lt
    inv_ref[...] = d
    basis_ref[:, m:] = dot3(basis_ref[:, m:], d * root, 1, 1)


def plans_kernel(root, ck, cl, scale, mine_ref, other_ref, lead_ref, ltu_ref, d_ref, s_ref, l_ref,
                 basis_ref, core_ref, w, sums_ref):
    m = w.shape[0]
    joined(sums_ref, mine_ref, other_ref)
    ll = sums_ref[:m, :]
    n22 = sums_ref[m:, :]
    load_gram(w, ll - lead_ref[7])
    a, l21u, av, l21v, xv = (lead_ref[i] for i in (0, 1, 4, 5, 6))
    d = d_ref[...]
    both = against(s_ref[...], av, xv)
    basis_ref[:, :m] = both[:, :m] * root
    basis_ref[:, m:] = l_ref[...] - both[:, m:]
    b = -dot(dot(d, l21u, 1, 0, HI), a, 1, 0, HI)
    core_ref[m:, m:] = (
        dot(b, ll, 1, 0, HI) * (1.0 / cl) + dot(d, n22, 1, 0, HI)
        - dot(ltu_ref[...], xv, 1, 0, HI) * (1.0 / ck)
    )
    core_ref[:m, :m] = dot(a, l21v, 1, 0, HI) * (scale / cl)
    core_ref[m:, :m] = dot(ltu_ref[...], av, 1, 1, HI) * (scale / ck)
    eliminate([w])
    ltv, dv = upper(w)
    basis_ref[:, m:] = dot3(basis_ref[:, m:], dv * root, 1, 1)
    core_ref[:m, m:] = dot(a, ltv, 1, 1, HI) * (scale / cl)
    core_ref[m:, m:] = dot(core_ref[m:, m:], dv, 1, 1, HI) * scale


def cost(units):
    return pl.CostEstimate(flops=0, bytes_accessed=units * 3_600_000, transcendentals=0)


def params(mib):
    return pltpu.CompilerParams(vmem_limit_bytes=mib << 20)


def local(cell_factor, sched_factor, core_matrix, rate_table, cell_well, sched_profile):
    cells_dev, rank = cell_factor.shape
    n_sched = sched_factor.shape[0]
    n = lax.axis_size("cell")
    n_cells = cells_dev * n
    profiles = rate_table.shape[1]
    me = lax.axis_index("cell")
    blk = n_sched // n
    bits = n.bit_length() - 1
    half = n // 2
    ck = PANEL_SCALE / n_sched
    cl = PANEL_SCALE / n_cells
    order_a = list(range(bits))
    order_b = [0, 2, 1] + order_a[3:] if bits > 2 else order_a

    def relative(j):
        return sum(((j >> (bits - 1 - i)) & 1) << bit for i, bit in enumerate(order_a))

    def slot_of(at):
        p = relative(at)
        return sum(((p >> bit) & 1) << (bits - 1 - i) for i, bit in enumerate(order_b) if i > 0)

    vmem = pl.BlockSpec(memory_space=pltpu.VMEM)
    hbm = pl.BlockSpec(memory_space=pltpu.HBM)
    anywhere = pl.BlockSpec(memory_space=pl.ANY)

    def shape(dtype, *dims):
        return jax.ShapeDtypeStruct(dims, dtype)

    part = shape(bf16, half, blk, rank)
    gram_half = shape(f32, rank + 8, rank)
    k, gram_send, gram, send_l, send_m, hold_l, hold_m = pl.pallas_call(
        lambda *refs: state_kernel(ck, cl, relative, slot_of, *refs),
        out_shape=(shape(f32, cells_dev, rank), gram_half, gram_half, part, part, part, part),
        in_specs=[hbm] * 6,
        out_specs=(vmem,) * 3 + (hbm,) * 4,
        scratch_shapes=[
            pltpu.VMEM((cells_dev, rank), bf16),
            pltpu.VMEM((n, blk, rank), bf16),
            pltpu.VMEM((rank, rank), f32),
            pltpu.VMEM(rate_table.shape, bf16),
            pltpu.VMEM((1, cells_dev), i32),
            pltpu.VMEM((n, 1, blk), i32),
            pltpu.VMEM((n, blk, cells_dev), bf16),
            pltpu.VMEM((rank, cells_dev), bf16),
            pltpu.VMEM((profiles, rank), f32),
            pltpu.VMEM((rank, cells_dev), f32),
            pltpu.VMEM((cells_dev, 2 * rank), bf16),
            pltpu.VMEM((2 * profiles, 2 * rank), bf16),
            pltpu.VMEM((n, blk, rank), bf16),
            pltpu.VMEM((n, blk, rank), bf16),
            pltpu.VMEM((2 * rank + 16, rank), f32),
            pltpu.SemaphoreType.DMA((6,)),
            pltpu.SemaphoreType.DMA((2, n)),
        ],
        compiler_params=params(60),
        name="state",
    )(
        cell_factor, sched_factor.reshape(n, blk, rank), core_matrix,
        rate_table, cell_well.reshape(1, cells_dev), sched_profile.reshape(n, 1, blk),
    )
    ss = dot(sched_factor, sched_factor, 0, 0)
    pair = pltpu.VMEM((rank, 2 * rank), f32)
    square = shape(f32, rank, rank)

    came_l, came_m = swap(send_l, 1, n), swap(send_m, 1, n)
    gram = gram + swap(gram_send, 1, n)
    quarter = half // 2
    block = (1, blk, rank)
    near = pl.BlockSpec(block, lambda j: (j, 0, 0))
    far = pl.BlockSpec(block, lambda j: (quarter + j, 0, 0))
    part = shape(bf16, quarter, blk, rank)
    send_l, hold_l, send_m, hold_m = pl.pallas_call(
        first_fold_kernel, grid=(quarter,), out_shape=(part,) * 4,
        in_specs=[near, far] * 4, out_specs=(near,) * 4, compiler_params=params(20), name="first_fold",
    )(hold_l, hold_l, came_l, came_l, hold_m, hold_m, came_m, came_m)

    def fold(step, send_l, hold_l, send_m, hold_m, came_l, came_m, after):
        part = shape(bf16, half >> (step + 1), blk, rank)
        return pl.pallas_call(
            fold_kernel, out_shape=(part,) * 4, in_specs=[vmem] * 4 + [anywhere], out_specs=(vmem,) * 4,
            compiler_params=params(16), name="fold",
        )(hold_l, came_l, hold_m, came_m, after)

    came_l, came_m = swap(send_l, 1 << order_a[1], n), swap(send_m, 1 << order_b[1], n)
    for bit in range(1, bits):
        gram = gram + swap(gram, 1 << bit, n)
    gram_other = swap(gram, 1, n)
    av = pl.pallas_call(
        plans_lead_kernel, out_shape=square, in_specs=[vmem, anywhere], out_specs=vmem,
        scratch_shapes=[pair], compiler_params=params(16), cost_estimate=cost(5), name="plans_lead",
    )(ss, hold_l)
    send_l, hold_l, send_m, hold_m = fold(1, send_l, hold_l, send_m, hold_m, came_l, came_m, av)
    for step in range(2, bits - 1):
        came_l = swap(send_l, 1 << order_a[step], n)
        came_m = swap(send_m, 1 << order_b[step], n)
        send_l, hold_l, send_m, hold_m = fold(step, send_l, hold_l, send_m, hold_m, came_l, came_m, av)
    came_l, came_m = swap(send_l, 1 << order_a[-1], n), swap(send_m, 1 << order_b[-1], n)
    lead = pl.pallas_call(
        lambda *refs: lead_kernel(cl / ck, *refs),
        out_shape=shape(f32, 8, rank, rank),
        in_specs=[vmem] * 3, out_specs=vmem,
        scratch_shapes=[pair, pltpu.VMEM((2 * rank + 16, rank), f32)],
        compiler_params=params(16), cost_estimate=cost(6), name="lead",
    )(gram, gram_other, av)
    basis_cells, ltu, d = pl.pallas_call(
        lambda *refs: cells_kernel(float(n_cells) ** 0.5, *refs),
        out_shape=(shape(f32, cells_dev, 2 * rank), square, square),
        in_specs=[vmem] * 3, out_specs=(vmem,) * 3, scratch_shapes=[pair],
        compiler_params=params(16), cost_estimate=cost(8), name="cells",
    )(lead, cell_factor, k)
    lt, sums_send, sums = pl.pallas_call(
        pair_kernel, out_shape=(shape(f32, blk, rank), square, square),
        in_specs=[vmem] * 4 + [anywhere], out_specs=(vmem,) * 3,
        scratch_shapes=[pltpu.VMEM((2 * rank, rank), f32)],
        compiler_params=params(16), name="pair",
    )(hold_l, came_l, hold_m, came_m, av)
    sums = sums + swap(sums_send, 1, n)
    dues = [lead] * (bits - 2) + [d]
    for bit, due in zip(range(1, bits), dues):
        sums = pl.pallas_call(
            add_kernel, out_shape=square, in_specs=[vmem] * 2 + [anywhere], out_specs=vmem,
            compiler_params=params(16), name="add",
        )(sums, swap(sums, 1 << bit, n), due)
    sums_other = swap(sums, 1, n)
    own = lax.dynamic_slice_in_dim(sched_factor, me * blk, blk, 0)
    scale = rank / (float(n_cells) * float(n_sched)) ** 0.5
    basis_sched, core_out = pl.pallas_call(
        lambda *refs: plans_kernel(float(n_sched) ** 0.5, ck, cl, scale, *refs),
        out_shape=(
            jax.ShapeDtypeStruct((blk, 2 * rank), f32),
            jax.ShapeDtypeStruct((2 * rank, 2 * rank), f32),
        ),
        in_specs=[vmem] * 7, out_specs=(vmem,) * 2,
        scratch_shapes=[pair, pltpu.VMEM((2 * rank, rank), f32)],
        compiler_params=params(16), name="plans",
    )(sums, sums_other, lead, ltu, d, own, lt)
    return (basis_cells, basis_sched, core_out)


def solution(mesh):
    return jax.shard_map(
        local,
        mesh=mesh,
        in_specs=(
            P(("group", "cell"), None),
            P("group", None),
            P("group", None),
            P(),
            P(("group", "cell")),
            P("group"),
        ),
        out_specs=(P(("group", "cell"), None), P(("group", "cell"), None), P("group", None)),
        check_vma=False,
    )
```
